128 devices in a mesh: group: 8 (over x, y_hi), fsdp: 16 (over y_lo, z, core).
Axes of the slice: x: 4, y: 4 (y_hi: 2, y_lo: 2; y = y_hi * 2 + y_lo), z: 4, core: 2. Of those that a mesh axis runs over, the one named last changes fastest.
Arguments:
- tokens: bfloat16 [65536, 8192], P(('group', 'fsdp')), may hold values from -60 to 60
- norm_gain: bfloat16 [8, 8192], P('group', 'fsdp'), may hold values from 0.099609375 to 1.8984375
- value_weight: bfloat16 [8, 8192, 512], P('group', 'fsdp'), may hold values from -0.125 to 0.125
- cotangent: bfloat16 [65536, 512], P(('group', 'fsdp')), may hold values from -0.59765625 to 0.59765625
- pseudo_grad: bfloat16 [8, 2048, 8192], P('group', 'fsdp'), may hold values from -6 to 6
- outer_params: float32 [2048, 8192], P('fsdp', 'group'), may hold values from -6 to 6
- momentum: float32 [2048, 8192], P('fsdp', 'group'), may hold values from -3 to 3
Outputs:
- values: bfloat16 [65536, 512], P(('group', 'fsdp'))
- token_grad: bfloat16 [65536, 8192], P(('group', 'fsdp'))
- weight_grad: float32 [8, 8192, 512], P('group', 'fsdp')
- gain_grad: float32 [8, 8192], P('group', 'fsdp')
- new_global: float32 [2048, 8192], P('fsdp', 'group')
- new_momentum: float32 [2048, 8192], P('fsdp', 'group')
- new_params: bfloat16 [2048, 8192], P('fsdp')
The draws below stay inside these ranges and needn't reach their ends.
All inputs are finite; a program needn't handle non-finite values.
Results may differ from the reference program's by a relative error of at most 0.012.
Values may be sent and summed in bfloat16 or wider, within the bound.
A program may use at most 192 MiB of HBM per device.

```python
import math
import jax
import jax.numpy as jnp
from jax import lax

D = 8192
KVW = 512
GROUP_TOK = 8192
TOKENS = 65536
FRAG = 2048
N_GROUP = 8


def draw_tokens(key, part):
    key = jax.random.fold_in(key, 7)
    row_key, col_key, entry_key = jax.random.split(key, 3)
    row_scale = jnp.exp(jax.random.uniform(row_key, (TOKENS, 1), jnp.float32) * math.log(10.0))
    col_scale = jnp.exp(jax.random.uniform(col_key, (1, D), jnp.float32) * math.log(10.0))
    entries = jnp.clip(jax.random.normal(entry_key, (TOKENS, D), jnp.float32), -6.0, 6.0)
    return (entries * row_scale * col_scale * 0.1).astype(jnp.bfloat16)


def with_spikes(result, stream_key, source, target, parts, factor):
    def block_of(dim):
        return (jnp.arange(result.shape[dim]) // (result.shape[dim] // parts)).reshape((-1,) + (1,) * (result.ndim - 1 - dim))

    near = jax.random.permutation(stream_key, parts)[block_of(target)]
    other_side = (block_of(target) + parts // 2) % parts
    return jnp.where((block_of(source) == near) | (block_of(source) == other_side), factor * result, result)


def block_scale(key, shape, cuts, low, top_value):
    def one(dim, blocks):
        steps = jax.random.uniform(jax.random.fold_in(jax.random.fold_in(key, 6), dim), (blocks,), jnp.float32, low / len(cuts), top_value / len(cuts))
        return jnp.repeat(jnp.exp(steps), shape[dim] // blocks).reshape((-1,) + (1,) * (len(shape) - dim - 1))

    level = one(*cuts[0])
    for cut in cuts[1:]:
        level = level * one(*cut)
    return level


def centred(stream_key, extent, spread, most, cuts=(), kind=jnp.bfloat16):
    drawn = jax.random.normal(stream_key, extent, jnp.float32) * spread
    if len(cuts) > 0:
        drawn = block_scale(stream_key, extent, cuts, -0.22, 0.18) * drawn
    return jnp.clip(drawn, min=-most, max=most).astype(kind)


def gaussian_with(own_key, shape, width, bound, pieces, heavy, held_as=jnp.bfloat16):
    result = width * jax.random.normal(own_key, shape, jnp.float32)
    if pieces:
        result = result * block_scale(own_key, shape, pieces, -0.22, 0.18)
    return jnp.clip(with_spikes(result, jax.random.fold_in(own_key, 3), *heavy), -bound, bound).astype(held_as)


def setup_inputs(seed: int = 0) -> dict:
    key_of = jax.random.split(jax.random.key(seed), 8)
    return {
        "tokens": draw_tokens(jax.random.fold_in(key_of[7], 71), 0),
        "norm_gain": jnp.clip(1.0 + 0.18 * jax.random.normal(key_of[1], (N_GROUP, D), jnp.float32), 0.099609375, 1.8984375).astype(jnp.bfloat16),
        "value_weight": centred(key_of[2], (N_GROUP, D, KVW), (D // 4) ** -0.5, 0.125, ((0, 8), (1, 16))),
        "cotangent": centred(key_of[3], (TOKENS, KVW), 0.1, 0.59765625, ((0, 128),)),
        "pseudo_grad": gaussian_with(key_of[4], (N_GROUP, FRAG, D), 1.0, 6.0, ((0, 8), (1, 16)), (0, 2, 8, 2.0)),
        "outer_params": centred(key_of[5], (FRAG, D), 1.0, 6.0, ((0, 16), (1, 8)), jnp.float32),
        "momentum": centred(key_of[6], (FRAG, D), 0.5, 3.0, ((0, 16), (1, 8)), jnp.float32),
    }


epsilon = 1e-05
outer_rate = 0.7
momentum_decay = 0.9

def group_pass(operands):
    group_tokens, group_gain, group_weight, group_cot = operands
    wide_tokens = group_tokens.astype(jnp.float32)
    inv_rms = lax.rsqrt(lax.optimization_barrier(jnp.mean(wide_tokens * wide_tokens, axis=1, keepdims=True)) + epsilon)
    scaled = wide_tokens * inv_rms
    gain_row = group_gain.astype(jnp.float32)[None, :]
    hidden = (scaled * gain_row).astype(jnp.bfloat16)
    values = jnp.dot(hidden, group_weight, preferred_element_type=jnp.float32).astype(jnp.bfloat16)
    hidden_grad = lax.dot_general(group_cot, group_weight, (((1,), (1,)), ((), ())), preferred_element_type=jnp.float32)
    weight_grad = lax.dot_general(hidden, group_cot, (((0,), (0,)), ((), ())), preferred_element_type=jnp.float32)
    gain_grad = lax.optimization_barrier(jnp.sum(scaled * hidden_grad, axis=0))
    gained = gain_row * hidden_grad
    token_grad = inv_rms * (gained - scaled * lax.optimization_barrier(jnp.mean(scaled * gained, axis=1, keepdims=True)))
    return (values, token_grad.astype(jnp.bfloat16), weight_grad, gain_grad)

def reference(tokens, norm_gain, value_weight, cotangent, pseudo_grad, outer_params, momentum):
    operands = (tokens.reshape(N_GROUP, GROUP_TOK, D), norm_gain, value_weight, cotangent.reshape(N_GROUP, GROUP_TOK, KVW))
    values, token_grad, weight_grad, gain_grad = lax.map(group_pass, operands)
    average = lax.optimization_barrier(jnp.sum(pseudo_grad.astype(jnp.float32), axis=0)) / N_GROUP
    new_momentum = momentum_decay * momentum + average
    new_global = outer_params - outer_rate * (average + momentum_decay * new_momentum)
    new_params = new_global.astype(jnp.bfloat16)
    return (values.reshape(TOKENS, KVW), token_grad.reshape(TOKENS, D), weight_grad, gain_grad, new_global, new_momentum, new_params)
```

```python
import functools

import jax
import jax.numpy as jnp
from jax import lax
from jax.experimental import pallas as pl
from jax.experimental.pallas import tpu as pltpu
from jax.sharding import PartitionSpec as P

epsilon = 1e-05
outer_rate = 0.7
momentum_decay = 0.9

F32 = jnp.float32
BF16 = jnp.bfloat16

D = 8192
T = 512
B = 512
K = 512
H = B // 2
N_FSDP = 16
ROWS = 128
SHARE = 1024
PARTS = 2
PR = ROWS // PARTS
K1 = 320
K2 = K - K1
CHUNK = 1024
N_CHUNK = D // CHUNK
N_COPIES = 96


def kernel(
    tok_hbm, gain_ref, w_hbm, cot_hbm, pg_hbm, op_hbm, mo_hbm,
    val_o, tg_o, wgr_o, gg_o, ng_o, nm_o, np_o,
    tok, sibtok, wall, gs, ry, ryz, rh0, rh1, rz0, rz1,
    w_v, wt, cot_v, cps, cott, acc, sq, inv_v, wgv,
    px, pown, pys, pyr, psum, op_v, mo_v, ng_v, nm_v, np_v, val_v,
    ssem, rsem, lsem,
):
    group = lax.axis_index("group")
    fs = lax.axis_index("fsdp")
    x, yh = group // 2, group % 2
    yl, z, c = fs // 8, (fs // 2) % 4, fs % 2

    def at(dx=0, dyh=0, dyl=0, dz=0, dc=0):
        return (
            ((x + dx) % 4) * 2 + (yh + dyh) % 2,
            ((yl + dyl) % 2) * 8 + ((z + dz) % 4) * 2 + (c + dc) % 2,
        )

    SIB, YP, ZP, ZM, Y2 = at(dc=1), at(dyl=1), at(dz=1), at(dz=3), at(dyh=1)
    XS = {1: at(dx=1), 3: at(dx=3), 2: at(dx=2)}

    def col(dy, dz, dc):
        owner = ((yl + dy) % 2) * 8 + ((z + dz) % 4) * 2 + (c + dc) % 2
        return pl.multiple_of(owner * B, B)

    def slot(dy, dz, dc):
        return dy * 8 + dz * 2 + dc

    started = []
    locals_ = []

    def send(src, dst, to):
        n = len(started)
        copy = pltpu.make_async_remote_copy(
            src_ref=src, dst_ref=dst, send_sem=ssem.at[n], recv_sem=rsem.at[n],
            device_id=to, device_id_type=pl.DeviceIdType.MESH,
        )
        copy.start()
        started.append(copy)
        return copy

    def local(src, dst):
        copy = pltpu.make_async_copy(src, dst, lsem.at[len(locals_)])
        copy.start()
        locals_.append(copy)
        return copy

    load_w = local(w_hbm.at[0], w_v)
    load_tok = [
        local(tok_hbm.at[:, pl.ds(i * CHUNK, CHUNK)], tok.at[:, pl.ds(i * CHUNK, CHUNK)])
        for i in range(N_CHUNK)
    ]
    load_cot = local(cot_hbm, cot_v)
    wide_cols = pl.ds(pl.multiple_of(x * 2 * SHARE, 2 * SHARE), 2 * SHARE)
    load_pg = local(pg_hbm.at[0, :, wide_cols], pown)
    load_op = local(op_hbm, op_v)
    load_mo = local(mo_hbm, mo_v)

    barrier = pltpu.get_barrier_semaphore()
    partners = [SIB, YP, ZP, ZM, Y2, XS[1], XS[3], XS[2]]
    for to in partners:
        pl.semaphore_signal(barrier, inc=1, device_id=to, device_id_type=pl.DeviceIdType.MESH)

    load_w.wait()
    gain_row = gain_ref[...].astype(F32)
    gain_col = jnp.transpose(jnp.broadcast_to(gain_row, (128, B)))
    wall[0] = (w_v[...].astype(F32) * jnp.concatenate([gain_col] * 4, axis=1)).astype(BF16)

    pl.semaphore_wait(barrier, len(partners))

    def half(s, h):
        return wall.at[s, pl.ds(h * H, H)]

    def along_z(dy):
        own = slot(dy, 0, 0)
        zp, zm = slot(dy, 3, 0), slot(dy, 1, 0)
        got = {}
        for k in range(2):
            got["p", 1 - k] = send(half(own, 1 - k), half(zp, 1 - k), ZP)
            got["m", k] = send(half(own, k), half(zm, k), ZM)
        return got

    def to_sibling(dy, dz):
        return send(wall.at[slot(dy, dz, 0)], wall.at[slot(dy, dz, 1)], SIB)

    sib = {}
    yp = [send(half(0, h), half(slot(1, 0, 0), h), YP) for h in range(2)]
    az = {0: along_z(0)}
    ORDER = [(dy, dz) for dz in (2, 1, 3, 0) for dy in (1, 0)]
    st = {}
    for dy, dz in ORDER[:4]:
        st[dy, dz] = send(
            tok_hbm.at[:, pl.ds(col(dy, dz, 1), B)], sibtok.at[dy * 4 + dz], SIB
        )
    sib[0, 0] = to_sibling(0, 0)
    for dy, dz in ORDER[4:]:
        st[dy, dz] = send(
            tok_hbm.at[:, pl.ds(col(dy, dz, 1), B)], sibtok.at[dy * 4 + dz], SIB
        )

    def rows(p):
        return pl.ds(p * PR, PR)

    xs = {}
    for p in range(PARTS):
        for dx in (1, 3, 2):
            theirs = pl.ds(pl.multiple_of(((x + dx) % 4) * 2 * SHARE, 2 * SHARE), 2 * SHARE)
            xs[p, dx] = send(pg_hbm.at[0, rows(p), theirs], px.at[p, dx - 1], XS[dx])

    sq[...] = jnp.zeros_like(sq)
    for i in range(N_CHUNK):
        load_tok[i].wait()

        def squares(r, _, i=i):
            rr = pl.ds(r * 64, 64)
            wide = tok[rr, pl.ds(i * CHUNK, CHUNK)].astype(F32)
            wide = wide * wide
            total = wide[:, :128]
            for l in range(1, CHUNK // 128):
                total = total + wide[:, l * 128:(l + 1) * 128]
            sq[rr, :] += total
            return 0

        lax.fori_loop(0, T // 64, squares, 0)
    load_cot.wait()
    inv = lax.rsqrt(jnp.sum(sq[...], axis=1, keepdims=True) * (1.0 / D) + epsilon)
    inv_v[...] = inv
    scaled_cot = cot_v[...].astype(F32) * inv
    cps[...] = scaled_cot.astype(BF16)
    cott[0] = jnp.transpose(scaled_cot).astype(BF16)
    ct = send(cott.at[0], cott.at[1], SIB)

    def products(dy, dz):
        st[dy, dz].wait_recv()
        own = jnp.dot(cott[0], tok[:, pl.ds(col(dy, dz, 0), B)], preferred_element_type=F32)
        other = jnp.dot(cott[1], sibtok[dy * 4 + dz], preferred_element_type=F32)
        gs[dy, dz] = (own + other).astype(BF16)

    SEG = {0: (0, 0, K1), 1: (0, K1, K2), 2: (1, K1, K2)}
    seg_rh0 = {0: rh0.at[0, :K1 // 2], 1: rh0.at[1, :K2 // 2], 2: rh0.at[2, :K2 // 2]}
    seg_rh1 = {0: rh1.at[0, :K1 // 2], 1: rh1.at[1, :K2 // 2], 2: rh1.at[2, :K2 // 2]}
    seg_rz0 = {0: rz0.at[0, :K1], 1: rz0.at[1, :K2], 2: rz0.at[2, :K2]}
    seg_rz1 = {0: rz1.at[0, :K1], 1: rz1.at[1, :K2], 2: rz1.at[2, :K2]}

    def far_halves(g):
        dy, r0, n = SEG[g]
        m = n // 2
        return (
            send(gs.at[dy, 2, pl.ds(r0, m)], seg_rh0[g], ZP),
            send(gs.at[dy, 2, pl.ds(r0 + m, m)], seg_rh1[g], ZM),
        )

    def add_into(ref, other):
        ref[...] = (ref[...].astype(F32) + other[...].astype(F32)).astype(BF16)

    def near_free(g):
        dy, r0, n = SEG[g]
        m = n // 2
        return [
            send(gs.at[dy, 1, pl.ds(r0 + m, m)], seg_rz0[g].at[pl.ds(m, m)], ZP),
            send(gs.at[dy, 3, pl.ds(r0, m)], seg_rz1[g].at[pl.ds(0, m)], ZM),
        ]

    def near_joined(g, far):
        dy, r0, n = SEG[g]
        m = n // 2
        far[0].wait_recv()
        add_into(gs.at[dy, 1, pl.ds(r0, m)], seg_rh0[g])
        a = send(gs.at[dy, 1, pl.ds(r0, m)], seg_rz0[g].at[pl.ds(0, m)], ZP)
        far[1].wait_recv()
        add_into(gs.at[dy, 3, pl.ds(r0 + m, m)], seg_rh1[g])
        b = send(gs.at[dy, 3, pl.ds(r0 + m, m)], seg_rz1[g].at[pl.ds(m, m)], ZM)
        return [a, b]

    def across_y(dz):
        return send(gs.at[1, dz, pl.ds(0, K1)], ry.at[dz], YP)

    def join_y(dz):
        rys[dz].wait_recv()
        add_into(gs.at[0, dz, pl.ds(0, K1)], ry.at[dz])

    rys, far = {}, {}
    ct.wait_recv()
    products(1, 2)
    rys[2] = across_y(2)
    products(0, 2)
    far[1], far[2] = far_halves(1), far_halves(2)
    for dy, dz in ORDER[2:]:
        products(dy, dz)

    acc[...] = jnp.zeros_like(acc)

    def forward(dy, dz, dc):
        acc[...] += jnp.dot(
            tok[:, pl.ds(col(dy, dz, dc), B)], wall[slot(dy, dz, dc)], preferred_element_type=F32
        )

    def far_forward(dy):
        az[dy]["m", 0].wait_recv()
        a = send(half(slot(dy, 1, 0), 0), half(slot(dy, 2, 0), 0), ZM)
        az[dy]["p", 1].wait_recv()
        b = send(half(slot(dy, 3, 0), 1), half(slot(dy, 2, 0), 1), ZP)
        return a, b

    def rest_of_near(dy):
        az[dy]["m", 1].wait_recv()
        sib[dy, 1] = to_sibling(dy, 1)
        az[dy]["p", 0].wait_recv()
        sib[dy, 3] = to_sibling(dy, 3)

    def rest_of_far(dy):
        for copy in afar[dy]:
            copy.wait_recv()
        sib[dy, 2] = to_sibling(dy, 2)

    afar = {}
    yp[0].wait_recv()
    yp[1].wait_recv()
    az[1] = along_z(1)
    afar[0] = far_forward(0)
    sib[1, 0] = to_sibling(1, 0)
    rest_of_near(0)
    forward(0, 0, 0)
    sib[0, 0].wait_recv()
    forward(0, 0, 1)

    other_cols = pl.ds(pl.multiple_of((1 - yh) * SHARE, SHARE), SHARE)
    own_cols = pl.ds(pl.multiple_of(yh * SHARE, SHARE), SHARE)

    def outer_sum(p):
        for dx in (1, 3, 2):
            xs[p, dx].wait_recv()

        def total(cols):
            t = pown[rows(p), cols].astype(F32)
            for k in range(3):
                t = t + px[p, k, :, cols].astype(F32)
            return t

        pys[p] = total(other_cols).astype(BF16)
        copy = send(pys.at[p], pyr.at[p], Y2)
        psum[p] = total(own_cols)
        return copy

    def share_cols(dyh):
        return pl.ds(pl.multiple_of((x * 2 + (yh + dyh) % 2) * SHARE, SHARE), SHARE)

    def outer_step(p):
        y2s[p].wait_recv()
        rr = rows(p)
        average = (psum[p] + pyr[p].astype(F32)) * 0.125
        new_momentum = momentum_decay * mo_v[rr] + average
        new_global = op_v[rr] - outer_rate * (average + momentum_decay * new_momentum)
        nm_v[rr] = new_momentum
        ng_v[rr] = new_global
        np_v[rr] = new_global.astype(BF16)
        place = np_o.at[rr, share_cols(0)]
        npy[p] = send(np_v.at[rr], place, Y2)
        for dx in (1, 3, 2):
            npx[p, dx] = send(np_v.at[rr], place, XS[dx])
        local(np_v.at[rr], place)
        local(nm_v.at[rr], nm_o.at[rr])
        local(ng_v.at[rr], ng_o.at[rr])

    def spread_params(p):
        npy[p].wait_recv()
        place = np_o.at[rows(p), share_cols(1)]
        for dx in (1, 3, 2):
            npf[p, dx] = send(place, place, XS[dx])

    y2s, npy, npx, npf = {}, {}, {}, {}
    load_pg.wait()
    load_op.wait()
    load_mo.wait()
    y2s[0] = outer_sum(0)
    rys[1] = across_y(1)
    forward(1, 0, 0)
    forward(0, 1, 0)
    forward(0, 3, 0)
    for s in ((1, 0), (0, 1), (0, 3)):
        sib[s].wait_recv()
        forward(*s, 1)
    wt[...] = jnp.transpose(w_v[...].astype(F32))
    y2s[1] = outer_sum(1)
    outer_step(0)
    rys[3] = across_y(3)

    join_y(2)
    afar[1] = far_forward(1)
    rest_of_near(1)
    far[0] = far_halves(0)
    near = {g: near_free(g) + near_joined(g, far[g]) for g in (2, 1)}
    forward(1, 1, 0)
    forward(1, 3, 0)
    join_y(1)
    rest_of_far(0)
    outer_step(1)
    rys[0] = across_y(0)
    forward(0, 2, 0)
    for s in ((1, 1), (1, 3), (0, 2)):
        sib[s].wait_recv()
        forward(*s, 1)
    spread_params(0)
    rest_of_far(1)
    forward(1, 2, 0)
    sib[1, 2].wait_recv()
    forward(1, 2, 1)

    inv = inv_v[...]
    acc_v = acc[...]
    val_v[...] = (acc_v * inv).astype(BF16)
    local(val_v, val_o)
    inner = jnp.sum(cot_v[...].astype(F32) * acc_v, axis=1, keepdims=True)
    inv_v[...] = inv * inv * inv * inner * (1.0 / D)

    def backward(s, _):
        owner = ((yl + s // 8) % 2) * 8 + ((z + (s // 2) % 4) % 4) * 2 + (c + s % 2) % 2
        cols = pl.ds(pl.multiple_of(owner * B, B), B)
        grad = lax.dot_general(
            cps[...], wall[s], (((1,), (1,)), ((), ())), preferred_element_type=F32
        )
        tok[:, cols] = (grad - tok[:, cols].astype(F32) * inv_v[...]).astype(BF16)
        pltpu.make_async_copy(tok.at[:, cols], tg_o.at[:, cols], lsem.at[40 + s]).start()
        return 0

    def backward_done(s, _):
        owner = ((yl + s // 8) % 2) * 8 + ((z + (s // 2) % 4) % 4) * 2 + (c + s % 2) % 2
        cols = pl.ds(pl.multiple_of(owner * B, B), B)
        pltpu.make_async_copy(tok.at[:, cols], tg_o.at[:, cols], lsem.at[40 + s]).wait()
        return 0

    lax.fori_loop(0, 8, backward, 0)
    join_y(3)
    near[0] = near_free(0)
    lax.fori_loop(8, 16, backward, 0)
    spread_params(1)
    near[0] = near[0] + near_joined(0, far[0])

    for copy in near[2]:
        copy.wait_recv()
    gs[1, 0, pl.ds(K1, K2)] = (
        gs[1, 0, pl.ds(K1, K2)].astype(F32)
        + seg_rz0[2][...].astype(F32)
        + seg_rz1[2][...].astype(F32)
    ).astype(BF16)
    rz = send(gs.at[1, 0, pl.ds(K1, K2)], ryz, YP)

    for copy in near[1]:
        copy.wait_recv()
    low = (
        gs[0, 0, pl.ds(K1, K2)].astype(F32)
        + seg_rz0[1][...].astype(F32)
        + seg_rz1[1][...].astype(F32)
    )
    rys[0].wait_recv()
    high = gs[0, 0, pl.ds(0, K1)].astype(F32) + ry[0].astype(F32)
    for copy in near[0]:
        copy.wait_recv()
    high = high + seg_rz0[0][...].astype(F32) + seg_rz1[0][...].astype(F32)
    rz.wait_recv()
    low = low + ryz[...].astype(F32)
    total = jnp.concatenate([high, low], axis=0)
    gg_o[...] = jnp.sum(wt[...] * total, axis=0, keepdims=True)
    wgv[...] = jnp.transpose(total * gain_row)
    local(wgv, wgr_o.at[0])

    for p in range(PARTS):
        for dx in (1, 3, 2):
            npx[p, dx].wait_recv()
            npf[p, dx].wait_recv()
    for copy in started:
        copy.wait_send()
    lax.fori_loop(0, 16, backward_done, 0)
    done = {id(v) for v in [load_w, load_cot, load_pg, load_op, load_mo, *load_tok]}
    for copy in locals_:
        if id(copy) not in done:
            copy.wait()


def shards(tokens, norm_gain, value_weight, cotangent, pseudo_grad, outer_params, momentum):
    hbm = pl.BlockSpec(memory_space=pl.ANY)
    vmem = pl.BlockSpec(memory_space=pltpu.VMEM)
    out = jax.ShapeDtypeStruct
    return tuple(
        pl.pallas_call(
            kernel,
            out_shape=(
                out((T, K), BF16),
                out((T, D), BF16),
                out((1, B, K), F32),
                out((1, B), F32),
                out((ROWS, SHARE), F32),
                out((ROWS, SHARE), F32),
                out((ROWS, D), BF16),
            ),
            in_specs=[hbm, vmem, hbm, hbm, hbm, hbm, hbm],
            out_specs=(hbm, hbm, hbm, vmem, hbm, hbm, hbm),
            scratch_shapes=[
                pltpu.VMEM((T, D), BF16),
                pltpu.VMEM((8, T, B), BF16),
                pltpu.VMEM((N_FSDP, B, K), BF16),
                pltpu.VMEM((2, 4, K, B), BF16),
                pltpu.VMEM((4, K1, B), BF16),
                pltpu.VMEM((K2, B), BF16),
                pltpu.VMEM((3, K1 // 2, B), BF16),
                pltpu.VMEM((3, K1 // 2, B), BF16),
                pltpu.VMEM((3, K1, B), BF16),
                pltpu.VMEM((3, K1, B), BF16),
                pltpu.VMEM((B, K), BF16),
                pltpu.VMEM((K, B), F32),
                pltpu.VMEM((T, K), BF16),
                pltpu.VMEM((T, K), BF16),
                pltpu.VMEM((2, K, T), BF16),
                pltpu.VMEM((T, K), F32),
                pltpu.VMEM((T, 128), F32),
                pltpu.VMEM((T, 1), F32),
                pltpu.VMEM((B, K), F32),
                pltpu.VMEM((PARTS, 3, PR, 2 * SHARE), BF16),
                pltpu.VMEM((ROWS, 2 * SHARE), BF16),
                pltpu.VMEM((PARTS, PR, SHARE), BF16),
                pltpu.VMEM((PARTS, PR, SHARE), BF16),
                pltpu.VMEM((PARTS, PR, SHARE), F32),
                pltpu.VMEM((ROWS, SHARE), F32),
                pltpu.VMEM((ROWS, SHARE), F32),
                pltpu.VMEM((ROWS, SHARE), F32),
                pltpu.VMEM((ROWS, SHARE), F32),
                pltpu.VMEM((ROWS, SHARE), BF16),
                pltpu.VMEM((T, K), BF16),
                pltpu.SemaphoreType.DMA((N_COPIES,)),
                pltpu.SemaphoreType.DMA((N_COPIES,)),
                pltpu.SemaphoreType.DMA((64,)),
            ],
            compiler_params=pltpu.CompilerParams(
                collective_id=0, has_side_effects=True, vmem_limit_bytes=60 << 20
            ),
            name="window",
        )(tokens, norm_gain, value_weight, cotangent, pseudo_grad, outer_params, momentum)
    )


def solution(mesh):
    placed = (
        P(("group", "fsdp"), None),
        P("group", "fsdp"),
        P("group", "fsdp", None),
        P(("group", "fsdp"), None),
        P("group", "fsdp", None),
        P("fsdp", "group"),
        P("fsdp", "group"),
    )
    return jax.shard_map(
        shards,
        mesh=mesh,
        in_specs=placed,
        out_specs=(
            P(("group", "fsdp"), None),
            P(("group", "fsdp"), None),
            P("group", "fsdp", None),
            P("group", "fsdp"),
            P("fsdp", "group"),
            P("fsdp", "group"),
            P("fsdp", None),
        ),
        check_vma=False,
    )
```

```python
import functools

import jax
import jax.numpy as jnp
from jax import lax
from jax.experimental import pallas as pl
from jax.experimental.pallas import tpu as pltpu
from jax.sharding import PartitionSpec as P

epsilon = 1e-05
outer_rate = 0.7
momentum_decay = 0.9

F32 = jnp.float32
BF16 = jnp.bfloat16

D = 8192
T = 512
B = 512
K = 512
H = B // 2
N_FSDP = 16
ROWS = 128
SHARE = 1024
PARTS = 2
PR = ROWS // PARTS
K1 = 352
K2 = K - K1
M1 = 176
M2 = 96
CHUNK = 1024
N_CHUNK = D // CHUNK
N_COPIES = 96


def kernel(
    tok_hbm, gain_ref, w_hbm, cot_hbm, pg_hbm, op_hbm, mo_hbm,
    val_v, tok, sum_v, rzp, rzm, ryz, wt, ng_v, nm_v, np_v,
    sibtok, wall, gs, ry, rh0, rh1, rz0, rz1,
    w_v, cot_v, cps, cott, acc, sq, inv_v,
    px, pown, pys, pyr, psum, op_v, mo_v,
    ssem, rsem, lsem,
):
    group = lax.axis_index("group")
    fs = lax.axis_index("fsdp")
    x, yh = group // 2, group % 2
    yl, z, c = fs // 8, (fs // 2) % 4, fs % 2

    def at(dx=0, dyh=0, dyl=0, dz=0, dc=0):
        return (
            ((x + dx) % 4) * 2 + (yh + dyh) % 2,
            ((yl + dyl) % 2) * 8 + ((z + dz) % 4) * 2 + (c + dc) % 2,
        )

    SIB, YP, ZP, ZM, Y2 = at(dc=1), at(dyl=1), at(dz=1), at(dz=3), at(dyh=1)
    XS = {1: at(dx=1), 3: at(dx=3), 2: at(dx=2)}

    def col(dy, dz, dc):
        owner = ((yl + dy) % 2) * 8 + ((z + dz) % 4) * 2 + (c + dc) % 2
        return pl.multiple_of(owner * B, B)

    def slot(dy, dz, dc):
        return dy * 8 + dz * 2 + dc

    started = []
    locals_ = []

    def send(src, dst, to):
        n = len(started)
        copy = pltpu.make_async_remote_copy(
            src_ref=src, dst_ref=dst, send_sem=ssem.at[n], recv_sem=rsem.at[n],
            device_id=to, device_id_type=pl.DeviceIdType.MESH,
        )
        copy.start()
        started.append(copy)
        return copy

    def local(src, dst):
        copy = pltpu.make_async_copy(src, dst, lsem.at[len(locals_)])
        copy.start()
        locals_.append(copy)
        return copy

    load_w = local(w_hbm.at[0], w_v)
    load_tok = [
        local(tok_hbm.at[:, pl.ds(i * CHUNK, CHUNK)], tok.at[:, pl.ds(i * CHUNK, CHUNK)])
        for i in range(N_CHUNK)
    ]
    load_cot = local(cot_hbm, cot_v)
    wide_cols = pl.ds(pl.multiple_of(x * 2 * SHARE, 2 * SHARE), 2 * SHARE)
    load_pg = local(pg_hbm.at[0, :, wide_cols], pown)
    load_op = local(op_hbm, op_v)
    load_mo = local(mo_hbm, mo_v)

    barrier = pltpu.get_barrier_semaphore()
    partners = [SIB, YP, ZP, ZM, Y2, XS[1], XS[3], XS[2]]
    for to in partners:
        pl.semaphore_signal(barrier, inc=1, device_id=to, device_id_type=pl.DeviceIdType.MESH)

    load_w.wait()
    gain_row = gain_ref[...].astype(F32)
    gain_col = jnp.transpose(jnp.broadcast_to(gain_row, (128, B)))
    wall[0] = (w_v[...].astype(F32) * jnp.concatenate([gain_col] * 4, axis=1)).astype(BF16)

    pl.semaphore_wait(barrier, len(partners))

    def half(s, h):
        return wall.at[s, pl.ds(h * H, H)]

    def along_z(dy):
        own = slot(dy, 0, 0)
        zp, zm = slot(dy, 3, 0), slot(dy, 1, 0)
        got = {}
        for k in range(2):
            got["p", 1 - k] = send(half(own, 1 - k), half(zp, 1 - k), ZP)
            got["m", k] = send(half(own, k), half(zm, k), ZM)
        return got

    def to_sibling(dy, dz):
        return send(wall.at[slot(dy, dz, 0)], wall.at[slot(dy, dz, 1)], SIB)

    sib = {}
    yp = [send(half(0, h), half(slot(1, 0, 0), h), YP) for h in range(2)]
    az = {0: along_z(0)}
    ORDER = [(dy, dz) for dz in (2, 1, 3, 0) for dy in (1, 0)]
    st = {}
    for dy, dz in ORDER[:4]:
        st[dy, dz] = send(
            tok_hbm.at[:, pl.ds(col(dy, dz, 1), B)], sibtok.at[dy * 4 + dz], SIB
        )
    sib[0, 0] = to_sibling(0, 0)
    for dy, dz in ORDER[4:]:
        st[dy, dz] = send(
            tok_hbm.at[:, pl.ds(col(dy, dz, 1), B)], sibtok.at[dy * 4 + dz], SIB
        )

    def rows(p):
        return pl.ds(p * PR, PR)

    xs = {}
    for p in range(PARTS):
        for dx in (1, 3, 2):
            theirs = pl.ds(pl.multiple_of(((x + dx) % 4) * 2 * SHARE, 2 * SHARE), 2 * SHARE)
            xs[p, dx] = send(pg_hbm.at[0, rows(p), theirs], px.at[p, dx - 1], XS[dx])

    sq[...] = jnp.zeros_like(sq)
    for i in range(N_CHUNK):
        load_tok[i].wait()

        def squares(r, _, i=i):
            rr = pl.ds(r * 64, 64)
            wide = tok[rr, pl.ds(i * CHUNK, CHUNK)].astype(F32)
            wide = wide * wide
            total = wide[:, :128]
            for l in range(1, CHUNK // 128):
                total = total + wide[:, l * 128:(l + 1) * 128]
            sq[rr, :] += total
            return 0

        lax.fori_loop(0, T // 64, squares, 0)
    load_cot.wait()
    inv = lax.rsqrt(jnp.sum(sq[...], axis=1, keepdims=True) * (1.0 / D) + epsilon)
    inv_v[...] = inv
    scaled_cot = cot_v[...].astype(F32) * inv
    cps[...] = scaled_cot.astype(BF16)
    cott[0] = jnp.transpose(scaled_cot).astype(BF16)
    ct = send(cott.at[0], cott.at[1], SIB)

    def products(dy, dz):
        st[dy, dz].wait_recv()
        own = jnp.dot(cott[0], tok[:, pl.ds(col(dy, dz, 0), B)], preferred_element_type=F32)
        other = jnp.dot(cott[1], sibtok[dy * 4 + dz], preferred_element_type=F32)
        gs[dy, dz] = (own + other).astype(BF16)

    SEG = {0: (0, 0, K1, M1), 1: (0, K1, K2, M2), 2: (1, K1, K2, M2)}
    seg_rh0 = {0: rh0.at[0, :M1], 1: rh0.at[1, :M2], 2: rh0.at[2, :M2]}
    seg_rh1 = {0: rh1.at[0, :K1 - M1], 1: rh1.at[1, :K2 - M2], 2: rh1.at[2, :K2 - M2]}
    seg_rz0 = {0: rzp, 1: rz0.at[0], 2: rz0.at[1]}
    seg_rz1 = {0: rzm, 1: rz1.at[0], 2: rz1.at[1]}

    def far_halves(g):
        dy, r0, n, m = SEG[g]
        return (
            send(gs.at[dy, 2, pl.ds(r0, m)], seg_rh0[g], ZP),
            send(gs.at[dy, 2, pl.ds(r0 + m, n - m)], seg_rh1[g], ZM),
        )

    def add_into(ref, other):
        ref[...] = (ref[...].astype(F32) + other[...].astype(F32)).astype(BF16)

    near = {0: [], 1: [], 2: []}

    def near_free(g, dz):
        dy, r0, n, m = SEG[g]
        if dz == 1:
            copy = send(
                gs.at[dy, 1, pl.ds(r0 + m, n - m)], seg_rz0[g].at[pl.ds(m, n - m)], ZP
            )
        else:
            copy = send(gs.at[dy, 3, pl.ds(r0, m)], seg_rz1[g].at[pl.ds(0, m)], ZM)
        near[g].append(copy)

    def near_joined(g, dz):
        dy, r0, n, m = SEG[g]
        far[g][0 if dz == 1 else 1].wait_recv()
        if dz == 1:
            add_into(gs.at[dy, 1, pl.ds(r0, m)], seg_rh0[g])
            copy = send(gs.at[dy, 1, pl.ds(r0, m)], seg_rz0[g].at[pl.ds(0, m)], ZP)
        else:
            add_into(gs.at[dy, 3, pl.ds(r0 + m, n - m)], seg_rh1[g])
            copy = send(
                gs.at[dy, 3, pl.ds(r0 + m, n - m)], seg_rz1[g].at[pl.ds(m, n - m)], ZM
            )
        near[g].append(copy)

    def across_y(dz):
        return send(gs.at[1, dz, pl.ds(0, K1)], ry.at[dz], YP)

    def join_y(dz):
        rys[dz].wait_recv()
        add_into(gs.at[0, dz, pl.ds(0, K1)], ry.at[dz])

    rys, far = {}, {}
    ct.wait_recv()
    products(1, 2)
    rys[2] = across_y(2)
    products(0, 2)
    far[1], far[2] = far_halves(1), far_halves(2)
    for dy, dz in ORDER[2:]:
        products(dy, dz)

    acc[...] = jnp.zeros_like(acc)

    def forward(dy, dz, dc):
        acc[...] += jnp.dot(
            tok[:, pl.ds(col(dy, dz, dc), B)], wall[slot(dy, dz, dc)], preferred_element_type=F32
        )

    def far_forward(dy):
        az[dy]["m", 0].wait_recv()
        a = send(half(slot(dy, 1, 0), 0), half(slot(dy, 2, 0), 0), ZM)
        az[dy]["p", 1].wait_recv()
        b = send(half(slot(dy, 3, 0), 1), half(slot(dy, 2, 0), 1), ZP)
        return a, b

    def rest_of_near(dy):
        az[dy]["m", 1].wait_recv()
        sib[dy, 1] = to_sibling(dy, 1)
        az[dy]["p", 0].wait_recv()
        sib[dy, 3] = to_sibling(dy, 3)

    def rest_of_far(dy):
        for copy in afar[dy]:
            copy.wait_recv()
        sib[dy, 2] = to_sibling(dy, 2)

    afar = {}
    yp[0].wait_recv()
    yp[1].wait_recv()
    az[1] = along_z(1)
    afar[0] = far_forward(0)
    sib[1, 0] = to_sibling(1, 0)
    rest_of_near(0)
    forward(0, 0, 0)
    sib[0, 0].wait_recv()
    forward(0, 0, 1)

    other_cols = pl.ds(pl.multiple_of((1 - yh) * SHARE, SHARE), SHARE)
    own_cols = pl.ds(pl.multiple_of(yh * SHARE, SHARE), SHARE)

    def outer_sum(p):
        for dx in (1, 3, 2):
            xs[p, dx].wait_recv()

        def total(cols):
            t = pown[rows(p), cols].astype(F32)
            for k in range(3):
                t = t + px[p, k, :, cols].astype(F32)
            return t

        pys[p] = total(other_cols).astype(BF16)
        copy = send(pys.at[p], pyr.at[p], Y2)
        psum[p] = total(own_cols)
        return copy

    def share_cols(dyh):
        return pl.ds(pl.multiple_of((x * 2 + (yh + dyh) % 2) * SHARE, SHARE), SHARE)

    def outer_step(p):
        y2s[p].wait_recv()
        rr = rows(p)
        average = (psum[p] + pyr[p].astype(F32)) * 0.125
        new_momentum = momentum_decay * mo_v[rr] + average
        new_global = op_v[rr] - outer_rate * (average + momentum_decay * new_momentum)
        nm_v[rr] = new_momentum
        ng_v[rr] = new_global
        np_v[rr, share_cols(0)] = new_global.astype(BF16)
        place = np_v.at[rr, share_cols(0)]
        npy[p] = send(place, place, Y2)
        for dx in (1, 3, 2):
            npx[p, dx] = send(place, place, XS[dx])

    def spread_params(p):
        npy[p].wait_recv()
        place = np_v.at[rows(p), share_cols(1)]
        for dx in (1, 3, 2):
            npf[p, dx] = send(place, place, XS[dx])

    y2s, npy, npx, npf = {}, {}, {}, {}
    load_pg.wait()
    load_op.wait()
    load_mo.wait()
    y2s[0] = outer_sum(0)
    rys[1] = across_y(1)
    forward(1, 0, 0)
    forward(0, 1, 0)
    forward(0, 3, 0)
    for s in ((1, 0), (0, 1), (0, 3)):
        sib[s].wait_recv()
        forward(*s, 1)
    wt[...] = jnp.transpose(w_v[...].astype(F32))
    y2s[1] = outer_sum(1)
    outer_step(0)
    rys[3] = across_y(3)

    join_y(2)
    afar[1] = far_forward(1)
    rest_of_near(1)
    far[0] = far_halves(0)
    for g in (2, 1):
        near_free(g, 1)
        near_free(g, 3)
        near_joined(g, 1)
        near_joined(g, 3)
    forward(1, 1, 0)
    forward(1, 3, 0)
    join_y(1)
    near_free(0, 1)
    rest_of_far(0)
    outer_step(1)
    rys[0] = across_y(0)
    forward(0, 2, 0)
    for s in ((1, 1), (1, 3), (0, 2)):
        sib[s].wait_recv()
        forward(*s, 1)
    spread_params(0)
    rest_of_far(1)
    forward(1, 2, 0)
    sib[1, 2].wait_recv()
    forward(1, 2, 1)

    def backward(s, _):
        owner = ((yl + s // 8) % 2) * 8 + ((z + (s // 2) % 4) % 4) * 2 + (c + s % 2) % 2
        cols = pl.ds(pl.multiple_of(owner * B, B), B)
        grad = lax.dot_general(
            cps[...], wall[s], (((1,), (1,)), ((), ())), preferred_element_type=F32
        )
        tok[:, cols] = (grad - tok[:, cols].astype(F32) * inv_v[...]).astype(BF16)
        return 0

    join_y(3)
    near_free(0, 3)
    near_joined(0, 1)
    near_joined(0, 3)
    inv = inv_v[...]
    acc_v = acc[...]
    val_v[...] = (acc_v * inv).astype(BF16)
    inner = jnp.sum(cot_v[...].astype(F32) * acc_v, axis=1, keepdims=True)
    inv_v[...] = inv * inv * inv * inner * (1.0 / D)

    lax.fori_loop(0, 8, backward, 0)
    spread_params(1)

    for copy in near[2]:
        copy.wait_recv()
    gs[1, 0, pl.ds(K1, K2)] = (
        gs[1, 0, pl.ds(K1, K2)].astype(F32)
        + seg_rz0[2][...].astype(F32)
        + seg_rz1[2][...].astype(F32)
    ).astype(BF16)
    rz = send(gs.at[1, 0, pl.ds(K1, K2)], ryz, YP)
    lax.fori_loop(8, 16, backward, 0)

    for copy in near[1]:
        copy.wait_recv()
    low = pl.ds(K1, K2)
    sum_v[low] = (
        gs[0, 0, low].astype(F32) + seg_rz0[1][...].astype(F32) + seg_rz1[1][...].astype(F32)
    )
    rys[0].wait_recv()
    high = pl.ds(0, K1)
    sum_v[high] = gs[0, 0, high].astype(F32) + ry[0].astype(F32)
    for p in range(PARTS):
        for dx in (1, 3, 2):
            npx[p, dx].wait_recv()
            npf[p, dx].wait_recv()
    for copy in near[0]:
        copy.wait_recv()
    rz.wait_recv()
    for copy in started:
        copy.wait_send()


def finish(
    gain_ref, val_v, tg_v, sum_v, rzp, rzm, ryz, wt, ng_v, nm_v, np_v,
    val_o, tg_o, wgr_o, gg_o, ng_o, nm_o, np_o, wgv, ggv, sems,
):
    copies = [
        pltpu.make_async_copy(src, dst, sems.at[n])
        for n, (src, dst) in enumerate(
            [(tg_v, tg_o), (np_v, np_o), (val_v, val_o), (ng_v, ng_o), (nm_v, nm_o)]
        )
    ]
    for copy in copies:
        copy.start()
    high = sum_v[:K1] + rzp[...].astype(F32) + rzm[...].astype(F32)
    low = sum_v[K1:] + ryz[...].astype(F32)
    total = jnp.concatenate([high, low], axis=0)
    wgv[...] = jnp.transpose(total * gain_ref[...].astype(F32))
    copies.append(pltpu.make_async_copy(wgv, wgr_o.at[0], sems.at[5]))
    copies[-1].start()
    ggv[...] = jnp.sum(wt[...] * total, axis=0, keepdims=True)
    copies.append(pltpu.make_async_copy(ggv, gg_o, sems.at[6]))
    copies[-1].start()
    for copy in copies:
        copy.wait()


def shards(tokens, norm_gain, value_weight, cotangent, pseudo_grad, outer_params, momentum):
    hbm = pl.BlockSpec(memory_space=pl.ANY)
    vmem = pl.BlockSpec(memory_space=pltpu.VMEM)
    out = jax.ShapeDtypeStruct
    held = pl.pallas_call(
        kernel,
        out_shape=(
            pltpu.VMEM((T, K), BF16),
            pltpu.VMEM((T, D), BF16),
            pltpu.VMEM((K, B), F32),
            pltpu.VMEM((K1, B), BF16),
            pltpu.VMEM((K1, B), BF16),
            pltpu.VMEM((K2, B), BF16),
            pltpu.VMEM((K, B), F32),
            pltpu.VMEM((ROWS, SHARE), F32),
            pltpu.VMEM((ROWS, SHARE), F32),
            pltpu.VMEM((ROWS, D), BF16),
        ),
        in_specs=[hbm, vmem, hbm, hbm, hbm, hbm, hbm],
        out_specs=(vmem,) * 10,
        scratch_shapes=[
            pltpu.VMEM((8, T, B), BF16),
            pltpu.VMEM((N_FSDP, B, K), BF16),
            pltpu.VMEM((2, 4, K, B), BF16),
            pltpu.VMEM((4, K1, B), BF16),
            pltpu.VMEM((3, M1, B), BF16),
            pltpu.VMEM((3, M1, B), BF16),
            pltpu.VMEM((2, K2, B), BF16),
            pltpu.VMEM((2, K2, B), BF16),
            pltpu.VMEM((B, K), BF16),
            pltpu.VMEM((T, K), BF16),
            pltpu.VMEM((T, K), BF16),
            pltpu.VMEM((2, K, T), BF16),
            pltpu.VMEM((T, K), F32),
            pltpu.VMEM((T, 128), F32),
            pltpu.VMEM((T, 1), F32),
            pltpu.VMEM((PARTS, 3, PR, 2 * SHARE), BF16),
            pltpu.VMEM((ROWS, 2 * SHARE), BF16),
            pltpu.VMEM((PARTS, PR, SHARE), BF16),
            pltpu.VMEM((PARTS, PR, SHARE), BF16),
            pltpu.VMEM((PARTS, PR, SHARE), F32),
            pltpu.VMEM((ROWS, SHARE), F32),
            pltpu.VMEM((ROWS, SHARE), F32),
            pltpu.SemaphoreType.DMA((N_COPIES,)),
            pltpu.SemaphoreType.DMA((N_COPIES,)),
            pltpu.SemaphoreType.DMA((16,)),
        ],
        compiler_params=pltpu.CompilerParams(
            collective_id=0, has_side_effects=True, vmem_limit_bytes=40 << 20
        ),
        name="window",
    )(tokens, norm_gain, value_weight, cotangent, pseudo_grad, outer_params, momentum)
    held = [pltpu.with_memory_space_constraint(v, pltpu.VMEM) for v in held]
    return tuple(
        pl.pallas_call(
            finish,
            out_shape=(
                out((T, K), BF16),
                out((T, D), BF16),
                out((1, B, K), F32),
                out((1, B), F32),
                out((ROWS, SHARE), F32),
                out((ROWS, SHARE), F32),
                out((ROWS, D), BF16),
            ),
            in_specs=[vmem] * 11,
            out_specs=(hbm,) * 7,
            scratch_shapes=[
                pltpu.VMEM((B, K), F32),
                pltpu.VMEM((1, B), F32),
                pltpu.SemaphoreType.DMA((8,)),
            ],
            compiler_params=pltpu.CompilerParams(vmem_limit_bytes=16 << 20),
            name="finish",
        )(norm_gain, *held)
    )


def solution(mesh):
    placed = (
        P(("group", "fsdp"), None),
        P("group", "fsdp"),
        P("group", "fsdp", None),
        P(("group", "fsdp"), None),
        P("group", "fsdp", None),
        P("fsdp", "group"),
        P("fsdp", "group"),
    )
    return jax.shard_map(
        shards,
        mesh=mesh,
        in_specs=placed,
        out_specs=(
            P(("group", "fsdp"), None),
            P(("group", "fsdp"), None),
            P("group", "fsdp", None),
            P("group", "fsdp"),
            P("fsdp", "group"),
            P("fsdp", "group"),
            P("fsdp", None),
        ),
        check_vma=False,
    )
```

```python
import functools

import jax
import jax.numpy as jnp
from jax import lax
from jax.experimental import pallas as pl
from jax.experimental.pallas import tpu as pltpu
from jax.sharding import PartitionSpec as P

epsilon = 1e-05
outer_rate = 0.7
momentum_decay = 0.9

F32 = jnp.float32
BF16 = jnp.bfloat16

D = 8192
T = 512
B = 512
K = 512
H = B // 2
N_FSDP = 16
ROWS = 128
SHARE = 1024
PARTS = 2
PR = ROWS // PARTS
K1 = 352
K2 = K - K1
M1 = 176
M2 = 96
CHUNK = 1024
N_CHUNK = D // CHUNK
N_COPIES = 96


def kernel(
    tok_hbm, gain_hbm, w_hbm, cot_hbm, pg_hbm, op_hbm, mo_hbm,
    val_v, tok, sum_v, ryo, rzp, rzm, ryz, wt, ng_v, nm_v, np_v, gain_v,
    sibtok, wall, gs, ry, rh0, rh1, rz0, rz1,
    w_v, cot_v, cps, cott, acc, sq, inv_v,
    px, pown, pys, pyr, psum, op_v, mo_v,
    ssem, rsem, lsem,
):
    group = lax.axis_index("group")
    fs = lax.axis_index("fsdp")
    x, yh = group // 2, group % 2
    yl, z, c = fs // 8, (fs // 2) % 4, fs % 2

    def at(dx=0, dyh=0, dyl=0, dz=0, dc=0):
        return (
            ((x + dx) % 4) * 2 + (yh + dyh) % 2,
            ((yl + dyl) % 2) * 8 + ((z + dz) % 4) * 2 + (c + dc) % 2,
        )

    SIB, YP, ZP, ZM, Y2 = at(dc=1), at(dyl=1), at(dz=1), at(dz=3), at(dyh=1)
    XS = {1: at(dx=1), 3: at(dx=3), 2: at(dx=2)}

    def col(dy, dz, dc):
        owner = ((yl + dy) % 2) * 8 + ((z + dz) % 4) * 2 + (c + dc) % 2
        return pl.multiple_of(owner * B, B)

    def slot(dy, dz, dc):
        return dy * 8 + dz * 2 + dc

    started = []
    locals_ = []

    def send(src, dst, to):
        n = len(started)
        copy = pltpu.make_async_remote_copy(
            src_ref=src, dst_ref=dst, send_sem=ssem.at[n], recv_sem=rsem.at[n],
            device_id=to, device_id_type=pl.DeviceIdType.MESH,
        )
        copy.start()
        started.append(copy)
        return copy

    def local(src, dst):
        copy = pltpu.make_async_copy(src, dst, lsem.at[len(locals_)])
        copy.start()
        locals_.append(copy)
        return copy

    barrier = pltpu.get_barrier_semaphore()
    partners = [SIB, YP, ZP, ZM, Y2, XS[1], XS[3], XS[2]]
    for to in partners:
        pl.semaphore_signal(barrier, inc=1, device_id=to, device_id_type=pl.DeviceIdType.MESH)

    load_w = local(w_hbm.at[0], w_v)
    load_gain = local(gain_hbm, gain_v)
    load_tok = [
        local(tok_hbm.at[:, pl.ds(i * CHUNK, CHUNK)], tok.at[:, pl.ds(i * CHUNK, CHUNK)])
        for i in range(N_CHUNK)
    ]
    load_cot = local(cot_hbm, cot_v)
    wide_cols = pl.ds(pl.multiple_of(x * 2 * SHARE, 2 * SHARE), 2 * SHARE)
    load_pg = local(pg_hbm.at[0, :, wide_cols], pown)
    load_op = local(op_hbm, op_v)
    load_mo = local(mo_hbm, mo_v)

    load_gain.wait()
    load_w.wait()
    gain_row = gain_v[...].astype(F32)
    gain_col = jnp.transpose(jnp.broadcast_to(gain_row, (128, B)))
    wall[0] = (w_v[...].astype(F32) * jnp.concatenate([gain_col] * 4, axis=1)).astype(BF16)

    pl.semaphore_wait(barrier, len(partners))

    def half(s, h):
        return wall.at[s, pl.ds(h * H, H)]

    def along_z(dy):
        own = slot(dy, 0, 0)
        zp, zm = slot(dy, 3, 0), slot(dy, 1, 0)
        got = {}
        for k in range(2):
            got["p", 1 - k] = send(half(own, 1 - k), half(zp, 1 - k), ZP)
            got["m", k] = send(half(own, k), half(zm, k), ZM)
        return got

    def to_sibling(dy, dz):
        return send(wall.at[slot(dy, dz, 0)], wall.at[slot(dy, dz, 1)], SIB)

    sib = {}
    yp = [send(half(0, h), half(slot(1, 0, 0), h), YP) for h in range(2)]
    az = {0: along_z(0)}
    ORDER = [(dy, dz) for dz in (2, 1, 3, 0) for dy in (1, 0)]
    st = {}
    for dy, dz in ORDER[:4]:
        st[dy, dz] = send(
            tok_hbm.at[:, pl.ds(col(dy, dz, 1), B)], sibtok.at[dy * 4 + dz], SIB
        )
    sib[0, 0] = to_sibling(0, 0)
    for dy, dz in ORDER[4:]:
        st[dy, dz] = send(
            tok_hbm.at[:, pl.ds(col(dy, dz, 1), B)], sibtok.at[dy * 4 + dz], SIB
        )

    def rows(p):
        return pl.ds(p * PR, PR)

    xs = {}
    for p in range(PARTS):
        for dx in (1, 3, 2):
            theirs = pl.ds(pl.multiple_of(((x + dx) % 4) * 2 * SHARE, 2 * SHARE), 2 * SHARE)
            xs[p, dx] = send(pg_hbm.at[0, rows(p), theirs], px.at[p, dx - 1], XS[dx])

    sq[...] = jnp.zeros_like(sq)
    for i in range(N_CHUNK):
        load_tok[i].wait()

        def squares(r, _, i=i):
            rr = pl.ds(r * 64, 64)
            wide = tok[rr, pl.ds(i * CHUNK, CHUNK)].astype(F32)
            wide = wide * wide
            total = wide[:, :128]
            for l in range(1, CHUNK // 128):
                total = total + wide[:, l * 128:(l + 1) * 128]
            sq[rr, :] += total
            return 0

        lax.fori_loop(0, T // 64, squares, 0)
    load_cot.wait()
    inv = lax.rsqrt(jnp.sum(sq[...], axis=1, keepdims=True) * (1.0 / D) + epsilon)
    inv_v[...] = inv
    scaled_cot = cot_v[...].astype(F32) * inv
    cps[...] = scaled_cot.astype(BF16)
    cott[0] = jnp.transpose(scaled_cot).astype(BF16)
    ct = send(cott.at[0], cott.at[1], SIB)

    def products(dy, dz):
        st[dy, dz].wait_recv()
        own = jnp.dot(cott[0], tok[:, pl.ds(col(dy, dz, 0), B)], preferred_element_type=F32)
        other = jnp.dot(cott[1], sibtok[dy * 4 + dz], preferred_element_type=F32)
        gs[dy, dz] = (own + other).astype(BF16)

    SEG = {0: (0, 0, K1, M1), 1: (0, K1, K2, M2), 2: (1, K1, K2, M2)}
    seg_rh0 = {0: rh0.at[0, :M1], 1: rh0.at[1, :M2], 2: rh0.at[2, :M2]}
    seg_rh1 = {0: rh1.at[0, :K1 - M1], 1: rh1.at[1, :K2 - M2], 2: rh1.at[2, :K2 - M2]}
    seg_rz0 = {0: rzp, 1: rz0.at[0], 2: rz0.at[1]}
    seg_rz1 = {0: rzm, 1: rz1.at[0], 2: rz1.at[1]}

    def far_halves(g):
        dy, r0, n, m = SEG[g]
        return (
            send(gs.at[dy, 2, pl.ds(r0, m)], seg_rh0[g], ZP),
            send(gs.at[dy, 2, pl.ds(r0 + m, n - m)], seg_rh1[g], ZM),
        )

    def add_into(ref, other):
        ref[...] = (ref[...].astype(F32) + other[...].astype(F32)).astype(BF16)

    near = {0: [], 1: [], 2: []}

    def near_free(g, dz):
        dy, r0, n, m = SEG[g]
        if dz == 1:
            copy = send(
                gs.at[dy, 1, pl.ds(r0 + m, n - m)], seg_rz0[g].at[pl.ds(m, n - m)], ZP
            )
        else:
            copy = send(gs.at[dy, 3, pl.ds(r0, m)], seg_rz1[g].at[pl.ds(0, m)], ZM)
        near[g].append(copy)

    def near_joined(g, dz):
        dy, r0, n, m = SEG[g]
        far[g][0 if dz == 1 else 1].wait_recv()
        if dz == 1:
            add_into(gs.at[dy, 1, pl.ds(r0, m)], seg_rh0[g])
            copy = send(gs.at[dy, 1, pl.ds(r0, m)], seg_rz0[g].at[pl.ds(0, m)], ZP)
        else:
            add_into(gs.at[dy, 3, pl.ds(r0 + m, n - m)], seg_rh1[g])
            copy = send(
                gs.at[dy, 3, pl.ds(r0 + m, n - m)], seg_rz1[g].at[pl.ds(m, n - m)], ZM
            )
        near[g].append(copy)

    def across_y(dz):
        there = ryo if dz == 0 else ry.at[dz - 1]
        return send(gs.at[1, dz, pl.ds(0, K1)], there, YP)

    def join_y(dz):
        rys[dz].wait_recv()
        add_into(gs.at[0, dz, pl.ds(0, K1)], ry.at[dz - 1])

    rys, far = {}, {}
    ct.wait_recv()
    products(1, 2)
    rys[2] = across_y(2)
    products(0, 2)
    far[1], far[2] = far_halves(1), far_halves(2)
    for dy, dz in ORDER[2:]:
        products(dy, dz)

    acc[...] = jnp.zeros_like(acc)

    def forward(dy, dz, dc):
        acc[...] += jnp.dot(
            tok[:, pl.ds(col(dy, dz, dc), B)], wall[slot(dy, dz, dc)], preferred_element_type=F32
        )

    def far_forward(dy):
        az[dy]["m", 0].wait_recv()
        a = send(half(slot(dy, 1, 0), 0), half(slot(dy, 2, 0), 0), ZM)
        az[dy]["p", 1].wait_recv()
        b = send(half(slot(dy, 3, 0), 1), half(slot(dy, 2, 0), 1), ZP)
        return a, b

    def rest_of_near(dy):
        az[dy]["m", 1].wait_recv()
        sib[dy, 1] = to_sibling(dy, 1)
        az[dy]["p", 0].wait_recv()
        sib[dy, 3] = to_sibling(dy, 3)

    def rest_of_far(dy):
        for copy in afar[dy]:
            copy.wait_recv()
        sib[dy, 2] = to_sibling(dy, 2)

    afar = {}
    yp[0].wait_recv()
    yp[1].wait_recv()
    az[1] = along_z(1)
    afar[0] = far_forward(0)
    sib[1, 0] = to_sibling(1, 0)
    rest_of_near(0)
    forward(0, 0, 0)
    sib[0, 0].wait_recv()
    forward(0, 0, 1)

    other_cols = pl.ds(pl.multiple_of((1 - yh) * SHARE, SHARE), SHARE)
    own_cols = pl.ds(pl.multiple_of(yh * SHARE, SHARE), SHARE)

    def outer_sum(p):
        for dx in (1, 3, 2):
            xs[p, dx].wait_recv()

        def total(cols):
            t = pown[rows(p), cols].astype(F32)
            for k in range(3):
                t = t + px[p, k, :, cols].astype(F32)
            return t

        pys[p] = total(other_cols).astype(BF16)
        copy = send(pys.at[p], pyr.at[p], Y2)
        psum[p] = total(own_cols)
        return copy

    def share_cols(dyh):
        return pl.ds(pl.multiple_of((x * 2 + (yh + dyh) % 2) * SHARE, SHARE), SHARE)

    def outer_step(p):
        y2s[p].wait_recv()
        rr = rows(p)
        average = (psum[p] + pyr[p].astype(F32)) * 0.125
        new_momentum = momentum_decay * mo_v[rr] + average
        new_global = op_v[rr] - outer_rate * (average + momentum_decay * new_momentum)
        nm_v[rr] = new_momentum
        ng_v[rr] = new_global
        np_v[rr, share_cols(0)] = new_global.astype(BF16)
        place = np_v.at[rr, share_cols(0)]
        npy[p] = send(place, place, Y2)
        for dx in (1, 3, 2):
            npx[p, dx] = send(place, place, XS[dx])

    def spread_params(p):
        npy[p].wait_recv()
        place = np_v.at[rows(p), share_cols(1)]
        for dx in (1, 3, 2):
            npf[p, dx] = send(place, place, XS[dx])

    y2s, npy, npx, npf = {}, {}, {}, {}
    load_pg.wait()
    load_op.wait()
    load_mo.wait()
    y2s[0] = outer_sum(0)
    rys[1] = across_y(1)
    forward(1, 0, 0)
    forward(0, 1, 0)
    forward(0, 3, 0)
    for s in ((1, 0), (0, 1), (0, 3)):
        sib[s].wait_recv()
        forward(*s, 1)
    wt[...] = jnp.transpose(w_v[...].astype(F32))
    y2s[1] = outer_sum(1)
    outer_step(0)
    rys[3] = across_y(3)

    join_y(2)
    afar[1] = far_forward(1)
    rest_of_near(1)
    far[0] = far_halves(0)
    for g in (2, 1):
        near_free(g, 1)
        near_free(g, 3)
        near_joined(g, 1)
        near_joined(g, 3)
    forward(1, 1, 0)
    forward(1, 3, 0)
    join_y(1)
    near_free(0, 1)
    rest_of_far(0)
    outer_step(1)
    rys[0] = across_y(0)
    forward(0, 2, 0)
    for s in ((1, 1), (1, 3), (0, 2)):
        sib[s].wait_recv()
        forward(*s, 1)
    spread_params(0)
    rest_of_far(1)
    forward(1, 2, 0)
    sib[1, 2].wait_recv()
    forward(1, 2, 1)

    def backward(s, _):
        owner = ((yl + s // 8) % 2) * 8 + ((z + (s // 2) % 4) % 4) * 2 + (c + s % 2) % 2
        cols = pl.ds(pl.multiple_of(owner * B, B), B)
        grad = lax.dot_general(
            cps[...], wall[s], (((1,), (1,)), ((), ())), preferred_element_type=F32
        )
        tok[:, cols] = (grad - tok[:, cols].astype(F32) * inv_v[...]).astype(BF16)
        return 0

    join_y(3)
    near_free(0, 3)
    near_joined(0, 1)
    near_joined(0, 3)
    inv = inv_v[...]
    acc_v = acc[...]
    val_v[...] = (acc_v * inv).astype(BF16)
    inner = jnp.sum(cot_v[...].astype(F32) * acc_v, axis=1, keepdims=True)
    inv_v[...] = inv * inv * inv * inner * (1.0 / D)

    lax.fori_loop(0, 8, backward, 0)
    spread_params(1)

    for copy in near[2]:
        copy.wait_recv()
    gs[1, 0, pl.ds(K1, K2)] = (
        gs[1, 0, pl.ds(K1, K2)].astype(F32)
        + seg_rz0[2][...].astype(F32)
        + seg_rz1[2][...].astype(F32)
    ).astype(BF16)
    rz = send(gs.at[1, 0, pl.ds(K1, K2)], ryz, YP)
    lax.fori_loop(8, 16, backward, 0)

    high, low = pl.ds(0, K1), pl.ds(K1, K2)
    sum_v[high] = gs[0, 0, high].astype(F32)
    for copy in near[1]:
        copy.wait_recv()
    sum_v[low] = (
        gs[0, 0, low].astype(F32) + seg_rz0[1][...].astype(F32) + seg_rz1[1][...].astype(F32)
    )
    for p in range(PARTS):
        for dx in (1, 3, 2):
            npx[p, dx].wait_recv()
    late = [rz, rys[0], *near[0], *(npf[1, dx] for dx in (1, 3, 2))]
    for copy in started:
        if not any(copy is other for other in late):
            copy.wait_send()
    for p in range(PARTS):
        for dx in (1, 3, 2):
            npf[p, dx].wait_recv()
    for copy in late[2:]:
        copy.wait_send()
    for copy in [*near[0], rys[0], rz]:
        copy.wait_recv()
    rys[0].wait_send()
    rz.wait_send()


def finish(
    val_v, tg_v, sum_v, ryo, rzp, rzm, ryz, wt, ng_v, nm_v, np_v, gain_v,
    val_o, tg_o, wgr_o, gg_o, ng_o, nm_o, np_o, wgv, ggv, sems,
):
    copies = [
        pltpu.make_async_copy(src, dst, sems.at[n])
        for n, (src, dst) in enumerate(
            [(tg_v, tg_o), (np_v, np_o), (val_v, val_o), (ng_v, ng_o), (nm_v, nm_o)]
        )
    ]
    for copy in copies:
        copy.start()
    high = sum_v[:K1] + ryo[...].astype(F32) + rzp[...].astype(F32) + rzm[...].astype(F32)
    low = sum_v[K1:] + ryz[...].astype(F32)
    total = jnp.concatenate([high, low], axis=0)
    wgv[...] = jnp.transpose(total * gain_v[...].astype(F32))
    copies.append(pltpu.make_async_copy(wgv, wgr_o.at[0], sems.at[5]))
    copies[-1].start()
    ggv[...] = jnp.sum(wt[...] * total, axis=0, keepdims=True)
    copies.append(pltpu.make_async_copy(ggv, gg_o, sems.at[6]))
    copies[-1].start()
    for copy in copies:
        copy.wait()


def shards(tokens, norm_gain, value_weight, cotangent, pseudo_grad, outer_params, momentum):
    hbm = pl.BlockSpec(memory_space=pl.ANY)
    vmem = pl.BlockSpec(memory_space=pltpu.VMEM)
    out = jax.ShapeDtypeStruct
    held = pl.pallas_call(
        kernel,
        out_shape=(
            pltpu.VMEM((T, K), BF16),
            pltpu.VMEM((T, D), BF16),
            pltpu.VMEM((K, B), F32),
            pltpu.VMEM((K1, B), BF16),
            pltpu.VMEM((K1, B), BF16),
            pltpu.VMEM((K1, B), BF16),
            pltpu.VMEM((K2, B), BF16),
            pltpu.VMEM((K, B), F32),
            pltpu.VMEM((ROWS, SHARE), F32),
            pltpu.VMEM((ROWS, SHARE), F32),
            pltpu.VMEM((ROWS, D), BF16),
            pltpu.VMEM((1, B), BF16),
        ),
        in_specs=[hbm] * 7,
        out_specs=(vmem,) * 12,
        scratch_shapes=[
            pltpu.VMEM((8, T, B), BF16),
            pltpu.VMEM((N_FSDP, B, K), BF16),
            pltpu.VMEM((2, 4, K, B), BF16),
            pltpu.VMEM((3, K1, B), BF16),
            pltpu.VMEM((3, M1, B), BF16),
            pltpu.VMEM((3, M1, B), BF16),
            pltpu.VMEM((2, K2, B), BF16),
            pltpu.VMEM((2, K2, B), BF16),
            pltpu.VMEM((B, K), BF16),
            pltpu.VMEM((T, K), BF16),
            pltpu.VMEM((T, K), BF16),
            pltpu.VMEM((2, K, T), BF16),
            pltpu.VMEM((T, K), F32),
            pltpu.VMEM((T, 128), F32),
            pltpu.VMEM((T, 1), F32),
            pltpu.VMEM((PARTS, 3, PR, 2 * SHARE), BF16),
            pltpu.VMEM((ROWS, 2 * SHARE), BF16),
            pltpu.VMEM((PARTS, PR, SHARE), BF16),
            pltpu.VMEM((PARTS, PR, SHARE), BF16),
            pltpu.VMEM((PARTS, PR, SHARE), F32),
            pltpu.VMEM((ROWS, SHARE), F32),
            pltpu.VMEM((ROWS, SHARE), F32),
            pltpu.SemaphoreType.DMA((N_COPIES,)),
            pltpu.SemaphoreType.DMA((N_COPIES,)),
            pltpu.SemaphoreType.DMA((16,)),
        ],
        compiler_params=pltpu.CompilerParams(
            collective_id=0, has_side_effects=True, vmem_limit_bytes=40 << 20
        ),
        name="window",
    )(tokens, norm_gain, value_weight, cotangent, pseudo_grad, outer_params, momentum)
    held = [pltpu.with_memory_space_constraint(v, pltpu.VMEM) for v in held]
    return tuple(
        pl.pallas_call(
            finish,
            out_shape=(
                out((T, K), BF16),
                out((T, D), BF16),
                out((1, B, K), F32),
                out((1, B), F32),
                out((ROWS, SHARE), F32),
                out((ROWS, SHARE), F32),
                out((ROWS, D), BF16),
            ),
            in_specs=[vmem] * 12,
            out_specs=(hbm,) * 7,
            scratch_shapes=[
                pltpu.VMEM((B, K), F32),
                pltpu.VMEM((1, B), F32),
                pltpu.SemaphoreType.DMA((8,)),
            ],
            compiler_params=pltpu.CompilerParams(vmem_limit_bytes=16 << 20),
            name="finish",
        )(*held)
    )


def solution(mesh):
    placed = (
        P(("group", "fsdp"), None),
        P("group", "fsdp"),
        P("group", "fsdp", None),
        P(("group", "fsdp"), None),
        P("group", "fsdp", None),
        P("fsdp", "group"),
        P("fsdp", "group"),
    )
    return jax.shard_map(
        shards,
        mesh=mesh,
        in_specs=placed,
        out_specs=(
            P(("group", "fsdp"), None),
            P(("group", "fsdp"), None),
            P("group", "fsdp", None),
            P("group", "fsdp"),
            P("fsdp", "group"),
            P("fsdp", "group"),
            P("fsdp", None),
        ),
        check_vma=False,
    )
```

```python
import functools

import jax
import jax.numpy as jnp
from jax import lax
from jax.experimental import pallas as pl
from jax.experimental.pallas import tpu as pltpu
from jax.sharding import PartitionSpec as P

epsilon = 1e-05
outer_rate = 0.7
momentum_decay = 0.9

F32 = jnp.float32
BF16 = jnp.bfloat16

D = 8192
T = 512
B = 512
K = 512
H = B // 2
N_FSDP = 16
ROWS = 128
SHARE = 1024
PARTS = 2
PR = ROWS // PARTS
K1 = 352
K2 = K - K1
M1 = 176
M2 = 96
SHIFT = 32
CHUNK = 1024
N_CHUNK = D // CHUNK
N_COPIES = 96


def kernel(
    tok_hbm, gain_hbm, w_hbm, cot_hbm, pg_hbm, op_hbm, mo_hbm,
    val_v, tok, sum_v, ryo, rzp, rzm, ryz, wt, ng_v, nm_v, np_v, gain_v,
    sibtok, wall, gs, ry, rh0, rh1, rz0, rz1,
    w_v, cot_v, cps, cott, acc, sq, inv_v,
    px, pown, pys, pyr, psum, op_v, mo_v,
    ssem, rsem, lsem,
):
    group = lax.axis_index("group")
    fs = lax.axis_index("fsdp")
    x, yh = group // 2, group % 2
    yl, z, c = fs // 8, (fs // 2) % 4, fs % 2

    def at(dx=0, dyh=0, dyl=0, dz=0, dc=0):
        return (
            ((x + dx) % 4) * 2 + (yh + dyh) % 2,
            ((yl + dyl) % 2) * 8 + ((z + dz) % 4) * 2 + (c + dc) % 2,
        )

    SIB, YP, ZP, ZM, Y2 = at(dc=1), at(dyl=1), at(dz=1), at(dz=3), at(dyh=1)
    XS = {1: at(dx=1), 3: at(dx=3), 2: at(dx=2)}

    def col(dy, dz, dc):
        owner = ((yl + dy) % 2) * 8 + ((z + dz) % 4) * 2 + (c + dc) % 2
        return pl.multiple_of(owner * B, B)

    def slot(dy, dz, dc):
        return dy * 8 + dz * 2 + dc

    started = []
    locals_ = []

    def send(src, dst, to, when=None, land=None):
        n = len(started)
        copy = pltpu.make_async_remote_copy(
            src_ref=src, dst_ref=dst, send_sem=ssem.at[n],
            recv_sem=rsem.at[n if land is None else land],
            device_id=to, device_id_type=pl.DeviceIdType.MESH,
        )
        if when is None:
            copy.start()
        else:
            pl.when(when)(copy.start)
        started.append((copy, when))
        return copy

    def local(src, dst):
        copy = pltpu.make_async_copy(src, dst, lsem.at[len(locals_)])
        copy.start()
        locals_.append(copy)
        return copy

    barrier = pltpu.get_barrier_semaphore()
    partners = [SIB, YP, ZP, ZM, Y2, XS[1], XS[3], XS[2]]
    for to in partners:
        pl.semaphore_signal(barrier, inc=1, device_id=to, device_id_type=pl.DeviceIdType.MESH)

    load_w = local(w_hbm.at[0], w_v)
    load_gain = local(gain_hbm, gain_v)
    load_tok = [
        local(tok_hbm.at[:, pl.ds(i * CHUNK, CHUNK)], tok.at[:, pl.ds(i * CHUNK, CHUNK)])
        for i in range(N_CHUNK)
    ]
    load_cot = local(cot_hbm, cot_v)
    wide_cols = pl.ds(pl.multiple_of(x * 2 * SHARE, 2 * SHARE), 2 * SHARE)
    load_pg = local(pg_hbm.at[0, :, wide_cols], pown)
    load_op = local(op_hbm, op_v)
    load_mo = local(mo_hbm, mo_v)

    load_gain.wait()
    load_w.wait()
    gain_row = gain_v[...].astype(F32)
    gain_col = jnp.transpose(jnp.broadcast_to(gain_row, (128, B)))
    wall[0] = (w_v[...].astype(F32) * jnp.concatenate([gain_col] * 4, axis=1)).astype(BF16)

    pl.semaphore_wait(barrier, len(partners))

    def half(s, h):
        return wall.at[s, pl.ds(h * H, H)]

    def along_z(dy):
        own = slot(dy, 0, 0)
        zp, zm = slot(dy, 3, 0), slot(dy, 1, 0)
        got = {}
        for k in range(2):
            got["p", 1 - k] = send(half(own, 1 - k), half(zp, 1 - k), ZP)
            got["m", k] = send(half(own, k), half(zm, k), ZM)
        return got

    def to_sibling(dy, dz):
        return send(wall.at[slot(dy, dz, 0)], wall.at[slot(dy, dz, 1)], SIB)

    sib = {}
    yp = [send(half(0, h), half(slot(1, 0, 0), h), YP) for h in range(2)]
    az = {0: along_z(0)}
    ORDER = [(dy, dz) for dz in (2, 1, 3, 0) for dy in (1, 0)]
    st = {}
    for dy, dz in ORDER[:4]:
        st[dy, dz] = send(
            tok_hbm.at[:, pl.ds(col(dy, dz, 1), B)], sibtok.at[dy * 4 + dz], SIB
        )
    sib[0, 0] = to_sibling(0, 0)
    for dy, dz in ORDER[4:]:
        st[dy, dz] = send(
            tok_hbm.at[:, pl.ds(col(dy, dz, 1), B)], sibtok.at[dy * 4 + dz], SIB
        )

    def rows(p):
        return pl.ds(p * PR, PR)

    xs = {}
    for p in range(PARTS):
        for dx in (1, 3, 2):
            theirs = pl.ds(pl.multiple_of(((x + dx) % 4) * 2 * SHARE, 2 * SHARE), 2 * SHARE)
            xs[p, dx] = send(pg_hbm.at[0, rows(p), theirs], px.at[p, dx - 1], XS[dx])

    sq[...] = jnp.zeros_like(sq)
    for i in range(N_CHUNK):
        load_tok[i].wait()

        def squares(r, _, i=i):
            rr = pl.ds(r * 64, 64)
            wide = tok[rr, pl.ds(i * CHUNK, CHUNK)].astype(F32)
            wide = wide * wide
            total = wide[:, :128]
            for l in range(1, CHUNK // 128):
                total = total + wide[:, l * 128:(l + 1) * 128]
            sq[rr, :] += total
            return 0

        lax.fori_loop(0, T // 64, squares, 0)
    load_cot.wait()
    inv = lax.rsqrt(jnp.sum(sq[...], axis=1, keepdims=True) * (1.0 / D) + epsilon)
    inv_v[...] = inv
    scaled_cot = cot_v[...].astype(F32) * inv
    cps[...] = scaled_cot.astype(BF16)
    cott[0] = jnp.transpose(scaled_cot).astype(BF16)
    ct = send(cott.at[0], cott.at[1], SIB)

    def products(dy, dz):
        st[dy, dz].wait_recv()
        own = jnp.dot(cott[0], tok[:, pl.ds(col(dy, dz, 0), B)], preferred_element_type=F32)
        other = jnp.dot(cott[1], sibtok[dy * 4 + dz], preferred_element_type=F32)
        gs[dy, dz] = (own + other).astype(BF16)

    SEG = {0: (0, 0, K1, M1), 1: (0, K1, K2, M2), 2: (1, K1, K2, M2)}
    seg_rh0 = {0: rh0.at[0, :M1], 1: rh0.at[1, :M2], 2: rh0.at[2, :M2]}
    seg_rh1 = {0: rh1.at[0, :K1 - M1], 1: rh1.at[1, :K2 - M2], 2: rh1.at[2, :K2 - M2]}
    seg_rz0 = {0: rzp, 1: rz0.at[0], 2: rz0.at[1]}
    seg_rz1 = {0: rzm, 1: rz1.at[0], 2: rz1.at[1]}

    def far_halves(g):
        dy, r0, n, m = SEG[g]
        return (
            send(gs.at[dy, 2, pl.ds(r0, m)], seg_rh0[g], ZP),
            send(gs.at[dy, 2, pl.ds(r0 + m, n - m)], seg_rh1[g], ZM),
        )

    def add_into(ref, other):
        ref[...] = (ref[...].astype(F32) + other[...].astype(F32)).astype(BF16)

    near = {0: [], 1: [], 2: []}

    def near_free(g, dz):
        dy, r0, n, m = SEG[g]
        if dz == 1:
            copy = send(
                gs.at[dy, 1, pl.ds(r0 + m, n - m)], seg_rz0[g].at[pl.ds(m, n - m)], ZP
            )
        else:
            copy = send(gs.at[dy, 3, pl.ds(r0, m)], seg_rz1[g].at[pl.ds(0, m)], ZM)
        near[g].append(copy)

    def near_joined(g, dz):
        dy, r0, n, m = SEG[g]
        far[g][0 if dz == 1 else 1].wait_recv()
        if dz == 1:
            add_into(gs.at[dy, 1, pl.ds(r0, m)], seg_rh0[g])
            copy = send(gs.at[dy, 1, pl.ds(r0, m)], seg_rz0[g].at[pl.ds(0, m)], ZP)
        else:
            add_into(gs.at[dy, 3, pl.ds(r0 + m, n - m)], seg_rh1[g])
            copy = send(
                gs.at[dy, 3, pl.ds(r0 + m, n - m)], seg_rz1[g].at[pl.ds(m, n - m)], ZM
            )
        near[g].append(copy)

    def across_y(dz):
        there = ryo if dz == 0 else ry.at[dz - 1]
        return send(gs.at[1, dz, pl.ds(0, K1)], there, YP)

    def join_y(dz):
        rys[dz].wait_recv()
        add_into(gs.at[0, dz, pl.ds(0, K1)], ry.at[dz - 1])

    rys, far = {}, {}
    ct.wait_recv()
    products(1, 2)
    rys[2] = across_y(2)
    products(0, 2)
    far[1], far[2] = far_halves(1), far_halves(2)
    for dy, dz in ORDER[2:]:
        products(dy, dz)

    acc[...] = jnp.zeros_like(acc)

    def forward(dy, dz, dc):
        acc[...] += jnp.dot(
            tok[:, pl.ds(col(dy, dz, dc), B)], wall[slot(dy, dz, dc)], preferred_element_type=F32
        )

    def part(dy, dz, r0, r1):
        return wall.at[slot(dy, dz, 0), pl.ds(r0, r1 - r0)]

    lo, hi = H - SHIFT, H + SHIFT
    middle = {}

    def far_forward(dy):
        az[dy]["m", 0].wait_recv()
        a = send(part(dy, 1, 0, lo), part(dy, 2, 0, lo), ZM)
        middle[dy, 0] = len(started)
        b = send(part(dy, 1, lo, H), part(dy, 2, lo, H), ZM, when=z != 3)
        az[dy]["p", 1].wait_recv()
        c = send(part(dy, 3, hi, B), part(dy, 2, hi, B), ZP)
        middle[dy, 1] = len(started)
        d = send(part(dy, 3, H, hi), part(dy, 2, H, hi), ZP, when=z != 3)
        return a, b, c, d

    def rest_of_near(dy):
        az[dy]["m", 1].wait_recv()
        send(part(dy, 1, H, hi), part(dy, 2, H, hi), ZM, when=z == 1, land=middle[dy, 1])
        sib[dy, 1] = to_sibling(dy, 1)
        az[dy]["p", 0].wait_recv()
        send(part(dy, 3, lo, H), part(dy, 2, lo, H), ZP, when=z == 1, land=middle[dy, 0])
        sib[dy, 3] = to_sibling(dy, 3)

    def rest_of_far(dy):
        for copy in afar[dy]:
            copy.wait_recv()
        sib[dy, 2] = to_sibling(dy, 2)

    afar = {}
    yp[0].wait_recv()
    yp[1].wait_recv()
    az[1] = along_z(1)
    afar[0] = far_forward(0)
    sib[1, 0] = to_sibling(1, 0)
    rest_of_near(0)
    forward(0, 0, 0)
    sib[0, 0].wait_recv()
    forward(0, 0, 1)

    other_cols = pl.ds(pl.multiple_of((1 - yh) * SHARE, SHARE), SHARE)
    own_cols = pl.ds(pl.multiple_of(yh * SHARE, SHARE), SHARE)

    def outer_sum(p):
        for dx in (1, 3, 2):
            xs[p, dx].wait_recv()

        def total(cols):
            t = pown[rows(p), cols].astype(F32)
            for k in range(3):
                t = t + px[p, k, :, cols].astype(F32)
            return t

        pys[p] = total(other_cols).astype(BF16)
        copy = send(pys.at[p], pyr.at[p], Y2)
        psum[p] = total(own_cols)
        return copy

    def share_cols(dyh):
        return pl.ds(pl.multiple_of((x * 2 + (yh + dyh) % 2) * SHARE, SHARE), SHARE)

    def outer_step(p):
        y2s[p].wait_recv()
        rr = rows(p)
        average = (psum[p] + pyr[p].astype(F32)) * 0.125
        new_momentum = momentum_decay * mo_v[rr] + average
        new_global = op_v[rr] - outer_rate * (average + momentum_decay * new_momentum)
        nm_v[rr] = new_momentum
        ng_v[rr] = new_global
        np_v[rr, share_cols(0)] = new_global.astype(BF16)
        place = np_v.at[rr, share_cols(0)]
        npy[p] = send(place, place, Y2)
        for dx in (1, 3, 2):
            npx[p, dx] = send(place, place, XS[dx])

    def spread_params(p):
        npy[p].wait_recv()
        place = np_v.at[rows(p), share_cols(1)]
        for dx in (1, 3, 2):
            npf[p, dx] = send(place, place, XS[dx])

    y2s, npy, npx, npf = {}, {}, {}, {}
    load_pg.wait()
    load_op.wait()
    load_mo.wait()
    y2s[0] = outer_sum(0)
    rys[1] = across_y(1)
    forward(1, 0, 0)
    forward(0, 1, 0)
    forward(0, 3, 0)
    for s in ((1, 0), (0, 1), (0, 3)):
        sib[s].wait_recv()
        forward(*s, 1)
    wt[...] = jnp.transpose(w_v[...].astype(F32))
    y2s[1] = outer_sum(1)
    outer_step(0)
    rys[3] = across_y(3)

    join_y(2)
    afar[1] = far_forward(1)
    rest_of_near(1)
    far[0] = far_halves(0)
    for g in (2, 1):
        near_free(g, 1)
        near_free(g, 3)
        near_joined(g, 1)
        near_joined(g, 3)
    forward(1, 1, 0)
    forward(1, 3, 0)
    join_y(1)
    near_free(0, 1)
    rest_of_far(0)
    outer_step(1)
    rys[0] = across_y(0)
    forward(0, 2, 0)
    for s in ((1, 1), (1, 3), (0, 2)):
        sib[s].wait_recv()
        forward(*s, 1)
    spread_params(0)
    rest_of_far(1)
    forward(1, 2, 0)
    sib[1, 2].wait_recv()
    forward(1, 2, 1)

    def backward(s, _):
        owner = ((yl + s // 8) % 2) * 8 + ((z + (s // 2) % 4) % 4) * 2 + (c + s % 2) % 2
        cols = pl.ds(pl.multiple_of(owner * B, B), B)
        grad = lax.dot_general(
            cps[...], wall[s], (((1,), (1,)), ((), ())), preferred_element_type=F32
        )
        tok[:, cols] = (grad - tok[:, cols].astype(F32) * inv_v[...]).astype(BF16)
        return 0

    join_y(3)
    near_free(0, 3)
    near_joined(0, 1)
    near_joined(0, 3)
    inv = inv_v[...]
    acc_v = acc[...]
    val_v[...] = (acc_v * inv).astype(BF16)
    inner = jnp.sum(cot_v[...].astype(F32) * acc_v, axis=1, keepdims=True)
    inv_v[...] = inv * inv * inv * inner * (1.0 / D)

    lax.fori_loop(0, 8, backward, 0)
    spread_params(1)

    for copy in near[2]:
        copy.wait_recv()
    gs[1, 0, pl.ds(K1, K2)] = (
        gs[1, 0, pl.ds(K1, K2)].astype(F32)
        + seg_rz0[2][...].astype(F32)
        + seg_rz1[2][...].astype(F32)
    ).astype(BF16)
    rz = send(gs.at[1, 0, pl.ds(K1, K2)], ryz, YP)
    lax.fori_loop(8, 16, backward, 0)

    high, low = pl.ds(0, K1), pl.ds(K1, K2)
    sum_v[high] = gs[0, 0, high].astype(F32)
    for copy in near[1]:
        copy.wait_recv()
    sum_v[low] = (
        gs[0, 0, low].astype(F32) + seg_rz0[1][...].astype(F32) + seg_rz1[1][...].astype(F32)
    )
    for p in range(PARTS):
        for dx in (1, 3, 2):
            npx[p, dx].wait_recv()
    late = [rz, rys[0], *near[0], *(npf[1, dx] for dx in (1, 3, 2))]
    for copy, when in started:
        if when is not None:
            pl.when(when)(copy.wait_send)
        elif not any(copy is other for other in late):
            copy.wait_send()
    for p in range(PARTS):
        for dx in (1, 3, 2):
            npf[p, dx].wait_recv()
    for copy in late[2:]:
        copy.wait_send()
    for copy in [*near[0], rys[0], rz]:
        copy.wait_recv()
    rys[0].wait_send()
    rz.wait_send()


def finish(
    val_v, tg_v, sum_v, ryo, rzp, rzm, ryz, wt, ng_v, nm_v, np_v, gain_v,
    val_o, tg_o, wgr_o, gg_o, ng_o, nm_o, np_o, wgv, ggv, sems,
):
    copies = [
        pltpu.make_async_copy(src, dst, sems.at[n])
        for n, (src, dst) in enumerate(
            [(tg_v, tg_o), (np_v, np_o), (val_v, val_o), (ng_v, ng_o), (nm_v, nm_o)]
        )
    ]
    for copy in copies:
        copy.start()
    high = sum_v[:K1] + ryo[...].astype(F32) + rzp[...].astype(F32) + rzm[...].astype(F32)
    low = sum_v[K1:] + ryz[...].astype(F32)
    total = jnp.concatenate([high, low], axis=0)
    wgv[...] = jnp.transpose(total * gain_v[...].astype(F32))
    copies.append(pltpu.make_async_copy(wgv, wgr_o.at[0], sems.at[5]))
    copies[-1].start()
    ggv[...] = jnp.sum(wt[...] * total, axis=0, keepdims=True)
    copies.append(pltpu.make_async_copy(ggv, gg_o, sems.at[6]))
    copies[-1].start()
    for copy in copies:
        copy.wait()


def shards(tokens, norm_gain, value_weight, cotangent, pseudo_grad, outer_params, momentum):
    hbm = pl.BlockSpec(memory_space=pl.ANY)
    vmem = pl.BlockSpec(memory_space=pltpu.VMEM)
    out = jax.ShapeDtypeStruct
    held = pl.pallas_call(
        kernel,
        out_shape=(
            pltpu.VMEM((T, K), BF16),
            pltpu.VMEM((T, D), BF16),
            pltpu.VMEM((K, B), F32),
            pltpu.VMEM((K1, B), BF16),
            pltpu.VMEM((K1, B), BF16),
            pltpu.VMEM((K1, B), BF16),
            pltpu.VMEM((K2, B), BF16),
            pltpu.VMEM((K, B), F32),
            pltpu.VMEM((ROWS, SHARE), F32),
            pltpu.VMEM((ROWS, SHARE), F32),
            pltpu.VMEM((ROWS, D), BF16),
            pltpu.VMEM((1, B), BF16),
        ),
        in_specs=[hbm] * 7,
        out_specs=(vmem,) * 12,
        scratch_shapes=[
            pltpu.VMEM((8, T, B), BF16),
            pltpu.VMEM((N_FSDP, B, K), BF16),
            pltpu.VMEM((2, 4, K, B), BF16),
            pltpu.VMEM((3, K1, B), BF16),
            pltpu.VMEM((3, M1, B), BF16),
            pltpu.VMEM((3, M1, B), BF16),
            pltpu.VMEM((2, K2, B), BF16),
            pltpu.VMEM((2, K2, B), BF16),
            pltpu.VMEM((B, K), BF16),
            pltpu.VMEM((T, K), BF16),
            pltpu.VMEM((T, K), BF16),
            pltpu.VMEM((2, K, T), BF16),
            pltpu.VMEM((T, K), F32),
            pltpu.VMEM((T, 128), F32),
            pltpu.VMEM((T, 1), F32),
            pltpu.VMEM((PARTS, 3, PR, 2 * SHARE), BF16),
            pltpu.VMEM((ROWS, 2 * SHARE), BF16),
            pltpu.VMEM((PARTS, PR, SHARE), BF16),
            pltpu.VMEM((PARTS, PR, SHARE), BF16),
            pltpu.VMEM((PARTS, PR, SHARE), F32),
            pltpu.VMEM((ROWS, SHARE), F32),
            pltpu.VMEM((ROWS, SHARE), F32),
            pltpu.SemaphoreType.DMA((N_COPIES,)),
            pltpu.SemaphoreType.DMA((N_COPIES,)),
            pltpu.SemaphoreType.DMA((16,)),
        ],
        compiler_params=pltpu.CompilerParams(
            collective_id=0, has_side_effects=True, vmem_limit_bytes=40 << 20
        ),
        name="window",
    )(tokens, norm_gain, value_weight, cotangent, pseudo_grad, outer_params, momentum)
    held = [pltpu.with_memory_space_constraint(v, pltpu.VMEM) for v in held]
    return tuple(
        pl.pallas_call(
            finish,
            out_shape=(
                out((T, K), BF16),
                out((T, D), BF16),
                out((1, B, K), F32),
                out((1, B), F32),
                out((ROWS, SHARE), F32),
                out((ROWS, SHARE), F32),
                out((ROWS, D), BF16),
            ),
            in_specs=[vmem] * 12,
            out_specs=(hbm,) * 7,
            scratch_shapes=[
                pltpu.VMEM((B, K), F32),
                pltpu.VMEM((1, B), F32),
                pltpu.SemaphoreType.DMA((8,)),
            ],
            compiler_params=pltpu.CompilerParams(vmem_limit_bytes=16 << 20),
            name="finish",
        )(*held)
    )


def solution(mesh):
    placed = (
        P(("group", "fsdp"), None),
        P("group", "fsdp"),
        P("group", "fsdp", None),
        P(("group", "fsdp"), None),
        P("group", "fsdp", None),
        P("fsdp", "group"),
        P("fsdp", "group"),
    )
    return jax.shard_map(
        shards,
        mesh=mesh,
        in_specs=placed,
        out_specs=(
            P(("group", "fsdp"), None),
            P(("group", "fsdp"), None),
            P("group", "fsdp", None),
            P("group", "fsdp"),
            P("fsdp", "group"),
            P("fsdp", "group"),
            P("fsdp", None),
        ),
        check_vma=False,
    )
```

```python
import functools

import jax
import jax.numpy as jnp
from jax import lax
from jax.experimental import pallas as pl
from jax.experimental.pallas import tpu as pltpu
from jax.sharding import PartitionSpec as P

epsilon = 1e-05
outer_rate = 0.7
momentum_decay = 0.9

F32 = jnp.float32
BF16 = jnp.bfloat16

D = 8192
T = 512
B = 512
K = 512
H = B // 2
N_FSDP = 16
ROWS = 128
SHARE = 1024
PARTS = 2
PR = ROWS // PARTS
K1 = 352
K2 = K - K1
M1 = 176
M2 = 96
SHIFT = 32
CHUNK = 1024
N_CHUNK = D // CHUNK
N_COPIES = 96


def kernel(
    tok_hbm, gain_hbm, w_hbm, cot_hbm, pg_hbm, op_hbm, mo_hbm,
    val_v, tok, sum_v, ryo, rzp, rzm, ryz, wt, ng_v, nm_v, np_v, gain_v,
    sibtok, wall, gs, ry, rh0, rh1, rz0, rz1,
    w_v, cot_v, cps, cott, acc, sq, inv_v,
    px, pown, pys, pyr, psum, op_v, mo_v,
    ssem, rsem, lsem,
):
    group = lax.axis_index("group")
    fs = lax.axis_index("fsdp")
    x, yh = group // 2, group % 2
    yl, z, c = fs // 8, (fs // 2) % 4, fs % 2

    def at(dx=0, dyh=0, dyl=0, dz=0, dc=0):
        return (
            ((x + dx) % 4) * 2 + (yh + dyh) % 2,
            ((yl + dyl) % 2) * 8 + ((z + dz) % 4) * 2 + (c + dc) % 2,
        )

    SIB, YP, ZP, ZM, Y2 = at(dc=1), at(dyl=1), at(dz=1), at(dz=3), at(dyh=1)
    XS = {1: at(dx=1), 3: at(dx=3), 2: at(dx=2)}

    def col(dy, dz, dc):
        owner = ((yl + dy) % 2) * 8 + ((z + dz) % 4) * 2 + (c + dc) % 2
        return pl.multiple_of(owner * B, B)

    def slot(dy, dz, dc):
        return dy * 8 + dz * 2 + dc

    started = []
    locals_ = []

    def send(src, dst, to, when=None, land=None):
        n = len(started)
        copy = pltpu.make_async_remote_copy(
            src_ref=src, dst_ref=dst, send_sem=ssem.at[n],
            recv_sem=rsem.at[n if land is None else land],
            device_id=to, device_id_type=pl.DeviceIdType.MESH,
        )
        if when is None:
            copy.start()
        else:
            pl.when(when)(copy.start)
        started.append((copy, when))
        return copy

    def local(src, dst):
        copy = pltpu.make_async_copy(src, dst, lsem.at[len(locals_)])
        copy.start()
        locals_.append(copy)
        return copy

    barrier = pltpu.get_barrier_semaphore()
    partners = [SIB, YP, ZP, ZM, Y2, XS[1], XS[3], XS[2]]
    for to in partners:
        pl.semaphore_signal(barrier, inc=1, device_id=to, device_id_type=pl.DeviceIdType.MESH)

    load_w = local(w_hbm.at[0], w_v)
    load_gain = local(gain_hbm, gain_v)
    load_tok = [
        local(tok_hbm.at[:, pl.ds(i * CHUNK, CHUNK)], tok.at[:, pl.ds(i * CHUNK, CHUNK)])
        for i in range(N_CHUNK)
    ]
    load_cot = local(cot_hbm, cot_v)
    wide_cols = pl.ds(pl.multiple_of(x * 2 * SHARE, 2 * SHARE), 2 * SHARE)
    load_pg = local(pg_hbm.at[0, :, wide_cols], pown)
    load_op = local(op_hbm, op_v)
    load_mo = local(mo_hbm, mo_v)

    load_gain.wait()
    load_w.wait()
    gain_row = gain_v[...].astype(F32)
    gain_col = jnp.transpose(jnp.broadcast_to(gain_row, (128, B)))
    wall[0] = (w_v[...].astype(F32) * jnp.concatenate([gain_col] * 4, axis=1)).astype(BF16)

    pl.semaphore_wait(barrier, len(partners))

    def half(s, h):
        return wall.at[s, pl.ds(h * H, H)]

    def along_z(dy):
        own = slot(dy, 0, 0)
        zp, zm = slot(dy, 3, 0), slot(dy, 1, 0)
        got = {}
        for k in range(2):
            got["p", 1 - k] = send(half(own, 1 - k), half(zp, 1 - k), ZP)
            got["m", k] = send(half(own, k), half(zm, k), ZM)
        return got

    def to_sibling(dy, dz):
        return send(wall.at[slot(dy, dz, 0)], wall.at[slot(dy, dz, 1)], SIB)

    sib = {}
    yp = [send(half(0, h), half(slot(1, 0, 0), h), YP) for h in range(2)]
    az = {0: along_z(0)}
    ORDER = [(dy, dz) for dz in (2, 1, 3, 0) for dy in (1, 0)]
    st = {}
    for dy, dz in ORDER[:4]:
        st[dy, dz] = send(
            tok_hbm.at[:, pl.ds(col(dy, dz, 1), B)], sibtok.at[dy * 4 + dz], SIB
        )
    sib[0, 0] = to_sibling(0, 0)
    for dy, dz in ORDER[4:]:
        st[dy, dz] = send(
            tok_hbm.at[:, pl.ds(col(dy, dz, 1), B)], sibtok.at[dy * 4 + dz], SIB
        )

    def rows(p):
        return pl.ds(p * PR, PR)

    xs = {}
    for p in range(PARTS):
        for dx in (1, 3, 2):
            theirs = pl.ds(pl.multiple_of(((x + dx) % 4) * 2 * SHARE, 2 * SHARE), 2 * SHARE)
            xs[p, dx] = send(pg_hbm.at[0, rows(p), theirs], px.at[p, dx - 1], XS[dx])

    sq[...] = jnp.zeros_like(sq)
    for i in range(N_CHUNK):
        load_tok[i].wait()

        def squares(r, _, i=i):
            rr = pl.ds(r * 64, 64)
            wide = tok[rr, pl.ds(i * CHUNK, CHUNK)].astype(F32)
            wide = wide * wide
            total = wide[:, :128]
            for l in range(1, CHUNK // 128):
                total = total + wide[:, l * 128:(l + 1) * 128]
            sq[rr, :] += total
            return 0

        lax.fori_loop(0, T // 64, squares, 0)
    load_cot.wait()
    inv = lax.rsqrt(jnp.sum(sq[...], axis=1, keepdims=True) * (1.0 / D) + epsilon)
    inv_v[...] = inv
    scaled_cot = cot_v[...].astype(F32) * inv
    cps[...] = scaled_cot.astype(BF16)
    cott[0] = jnp.transpose(scaled_cot).astype(BF16)
    ct = send(cott.at[0], cott.at[1], SIB)

    def products(dy, dz):
        st[dy, dz].wait_recv()
        own = jnp.dot(cott[0], tok[:, pl.ds(col(dy, dz, 0), B)], preferred_element_type=F32)
        other = jnp.dot(cott[1], sibtok[dy * 4 + dz], preferred_element_type=F32)
        gs[dy, dz] = (own + other).astype(BF16)

    SEG = {0: (0, 0, K1, M1), 1: (0, K1, K2, M2), 2: (1, K1, K2, M2)}
    seg_rh0 = {0: rh0.at[0, :M1], 1: rh0.at[1, :M2], 2: rh0.at[2, :M2]}
    seg_rh1 = {0: rh1.at[0, :K1 - M1], 1: rh1.at[1, :K2 - M2], 2: rh1.at[2, :K2 - M2]}
    seg_rz0 = {0: rzp, 1: rz0.at[0], 2: rz0.at[1]}
    seg_rz1 = {0: rzm, 1: rz1.at[0], 2: rz1.at[1]}

    def far_halves(g):
        dy, r0, n, m = SEG[g]
        return (
            send(gs.at[dy, 2, pl.ds(r0, m)], seg_rh0[g], ZP),
            send(gs.at[dy, 2, pl.ds(r0 + m, n - m)], seg_rh1[g], ZM),
        )

    def add_into(ref, other):
        ref[...] = (ref[...].astype(F32) + other[...].astype(F32)).astype(BF16)

    near = {0: [], 1: [], 2: []}

    def near_free(g, dz):
        dy, r0, n, m = SEG[g]
        if dz == 1:
            copy = send(
                gs.at[dy, 1, pl.ds(r0 + m, n - m)], seg_rz0[g].at[pl.ds(m, n - m)], ZP
            )
        else:
            copy = send(gs.at[dy, 3, pl.ds(r0, m)], seg_rz1[g].at[pl.ds(0, m)], ZM)
        near[g].append(copy)

    def near_joined(g, dz):
        dy, r0, n, m = SEG[g]
        far[g][0 if dz == 1 else 1].wait_recv()
        if dz == 1:
            add_into(gs.at[dy, 1, pl.ds(r0, m)], seg_rh0[g])
            copy = send(gs.at[dy, 1, pl.ds(r0, m)], seg_rz0[g].at[pl.ds(0, m)], ZP)
        else:
            add_into(gs.at[dy, 3, pl.ds(r0 + m, n - m)], seg_rh1[g])
            copy = send(
                gs.at[dy, 3, pl.ds(r0 + m, n - m)], seg_rz1[g].at[pl.ds(m, n - m)], ZM
            )
        near[g].append(copy)

    def across_y(dz):
        there = ryo if dz == 0 else ry.at[dz - 1]
        return send(gs.at[1, dz, pl.ds(0, K1)], there, YP)

    def join_y(dz):
        rys[dz].wait_recv()
        add_into(gs.at[0, dz, pl.ds(0, K1)], ry.at[dz - 1])

    rys, far = {}, {}
    ct.wait_recv()
    products(1, 2)
    rys[2] = across_y(2)
    products(0, 2)
    far[1], far[2] = far_halves(1), far_halves(2)
    for dy, dz in ORDER[2:]:
        products(dy, dz)

    acc[...] = jnp.zeros_like(acc)

    def forward(dy, dz, dc):
        acc[...] += jnp.dot(
            tok[:, pl.ds(col(dy, dz, dc), B)], wall[slot(dy, dz, dc)], preferred_element_type=F32
        )

    def part(dy, dz, r0, r1):
        return wall.at[slot(dy, dz, 0), pl.ds(r0, r1 - r0)]

    lo, hi = H - SHIFT, H + SHIFT
    middle = {}

    def far_forward(dy):
        az[dy]["m", 0].wait_recv()
        a = send(part(dy, 1, 0, lo), part(dy, 2, 0, lo), ZM)
        middle[dy, 0] = len(started)
        b = send(part(dy, 1, lo, H), part(dy, 2, lo, H), ZM, when=z != 3)
        az[dy]["p", 1].wait_recv()
        c = send(part(dy, 3, hi, B), part(dy, 2, hi, B), ZP)
        middle[dy, 1] = len(started)
        d = send(part(dy, 3, H, hi), part(dy, 2, H, hi), ZP, when=z != 3)
        return a, b, c, d

    def rest_of_near(dy):
        az[dy]["m", 1].wait_recv()
        send(part(dy, 1, H, hi), part(dy, 2, H, hi), ZM, when=z == 1, land=middle[dy, 1])
        sib[dy, 1] = to_sibling(dy, 1)
        az[dy]["p", 0].wait_recv()
        send(part(dy, 3, lo, H), part(dy, 2, lo, H), ZP, when=z == 1, land=middle[dy, 0])
        sib[dy, 3] = to_sibling(dy, 3)

    def rest_of_far(dy):
        for copy in afar[dy]:
            copy.wait_recv()
        sib[dy, 2] = to_sibling(dy, 2)

    afar = {}
    yp[0].wait_recv()
    yp[1].wait_recv()
    az[1] = along_z(1)
    afar[0] = far_forward(0)
    sib[1, 0] = to_sibling(1, 0)
    rest_of_near(0)
    forward(0, 0, 0)
    sib[0, 0].wait_recv()
    forward(0, 0, 1)

    other_cols = pl.ds(pl.multiple_of((1 - yh) * SHARE, SHARE), SHARE)
    own_cols = pl.ds(pl.multiple_of(yh * SHARE, SHARE), SHARE)

    def outer_sum(p):
        for dx in (1, 3, 2):
            xs[p, dx].wait_recv()

        def total(cols):
            t = pown[rows(p), cols].astype(F32)
            for k in range(3):
                t = t + px[p, k, :, cols].astype(F32)
            return t

        pys[p] = total(other_cols).astype(BF16)
        copy = send(pys.at[p], pyr.at[p], Y2)
        psum[p] = total(own_cols)
        return copy

    def share_cols(dyh):
        return pl.ds(pl.multiple_of((x * 2 + (yh + dyh) % 2) * SHARE, SHARE), SHARE)

    def outer_step(p):
        y2s[p].wait_recv()
        rr = rows(p)
        average = (psum[p] + pyr[p].astype(F32)) * 0.125
        new_momentum = momentum_decay * mo_v[rr] + average
        new_global = op_v[rr] - outer_rate * (average + momentum_decay * new_momentum)
        nm_v[rr] = new_momentum
        ng_v[rr] = new_global
        np_v[rr, share_cols(0)] = new_global.astype(BF16)
        place = np_v.at[rr, share_cols(0)]
        npy[p] = send(place, place, Y2)
        for dx in (1, 3, 2):
            npx[p, dx] = send(place, place, XS[dx])

    def spread_params(p):
        npy[p].wait_recv()
        place = np_v.at[rows(p), share_cols(1)]
        for dx in (1, 3, 2):
            npf[p, dx] = send(place, place, XS[dx])

    y2s, npy, npx, npf = {}, {}, {}, {}
    load_pg.wait()
    load_op.wait()
    load_mo.wait()
    y2s[0] = outer_sum(0)
    rys[1] = across_y(1)
    forward(1, 0, 0)
    forward(0, 1, 0)
    forward(0, 3, 0)
    for s in ((1, 0), (0, 1), (0, 3)):
        sib[s].wait_recv()
        forward(*s, 1)
    wt[...] = jnp.transpose(w_v[...].astype(F32))
    y2s[1] = outer_sum(1)
    outer_step(0)
    rys[3] = across_y(3)

    join_y(2)
    afar[1] = far_forward(1)
    rest_of_near(1)
    far[0] = far_halves(0)
    for g in (2, 1):
        near_free(g, 1)
        near_free(g, 3)
        near_joined(g, 1)
        near_joined(g, 3)
    forward(1, 1, 0)
    forward(1, 3, 0)
    join_y(1)
    near_free(0, 1)
    rest_of_far(0)
    outer_step(1)
    rys[0] = across_y(0)
    forward(0, 2, 0)
    for s in ((1, 1), (1, 3), (0, 2)):
        sib[s].wait_recv()
        forward(*s, 1)
    spread_params(0)
    rest_of_far(1)
    forward(1, 2, 0)
    sib[1, 2].wait_recv()
    forward(1, 2, 1)

    def backward(s, _):
        owner = ((yl + s // 8) % 2) * 8 + ((z + (s // 2) % 4) % 4) * 2 + (c + s % 2) % 2
        cols = pl.ds(pl.multiple_of(owner * B, B), B)
        grad = lax.dot_general(
            cps[...], wall[s], (((1,), (1,)), ((), ())), preferred_element_type=F32
        )
        tok[:, cols] = (grad - tok[:, cols].astype(F32) * inv_v[...]).astype(BF16)
        return 0

    join_y(3)
    near_free(0, 3)
    near_joined(0, 1)
    near_joined(0, 3)
    inv = inv_v[...]
    acc_v = acc[...]
    val_v[...] = (acc_v * inv).astype(BF16)
    inner = jnp.sum(cot_v[...].astype(F32) * acc_v, axis=1, keepdims=True)
    inv_v[...] = inv * inv * inv * inner * (1.0 / D)

    lax.fori_loop(0, 3, backward, 0)
    spread_params(1)
    lax.fori_loop(3, 8, backward, 0)

    for copy in near[2]:
        copy.wait_recv()
    gs[1, 0, pl.ds(K1, K2)] = (
        gs[1, 0, pl.ds(K1, K2)].astype(F32)
        + seg_rz0[2][...].astype(F32)
        + seg_rz1[2][...].astype(F32)
    ).astype(BF16)
    rz = send(gs.at[1, 0, pl.ds(K1, K2)], ryz, YP)
    lax.fori_loop(8, 16, backward, 0)

    high, low = pl.ds(0, K1), pl.ds(K1, K2)
    sum_v[high] = gs[0, 0, high].astype(F32)
    for copy in near[1]:
        copy.wait_recv()
    sum_v[low] = (
        gs[0, 0, low].astype(F32) + seg_rz0[1][...].astype(F32) + seg_rz1[1][...].astype(F32)
    )
    for p in range(PARTS):
        for dx in (1, 3, 2):
            npx[p, dx].wait_recv()
    late = [rz, rys[0], *near[0], *(npf[1, dx] for dx in (1, 3, 2))]
    for copy, when in started:
        if when is not None:
            pl.when(when)(copy.wait_send)
        elif not any(copy is other for other in late):
            copy.wait_send()
    for p in range(PARTS):
        for dx in (1, 3, 2):
            npf[p, dx].wait_recv()
    for copy in late[2:]:
        copy.wait_send()
    for copy in [*near[0], rys[0], rz]:
        copy.wait_recv()
    rys[0].wait_send()
    rz.wait_send()


def finish(
    val_v, tg_v, sum_v, ryo, rzp, rzm, ryz, wt, ng_v, nm_v, np_v, gain_v,
    val_o, tg_o, wgr_o, gg_o, ng_o, nm_o, np_o, wgv, ggv, sems,
):
    copies = [
        pltpu.make_async_copy(src, dst, sems.at[n])
        for n, (src, dst) in enumerate(
            [(tg_v, tg_o), (np_v, np_o), (val_v, val_o), (ng_v, ng_o), (nm_v, nm_o)]
        )
    ]
    for copy in copies:
        copy.start()
    high = sum_v[:K1] + ryo[...].astype(F32) + rzp[...].astype(F32) + rzm[...].astype(F32)
    low = sum_v[K1:] + ryz[...].astype(F32)
    total = jnp.concatenate([high, low], axis=0)
    wgv[...] = jnp.transpose(total * gain_v[...].astype(F32))
    copies.append(pltpu.make_async_copy(wgv, wgr_o.at[0], sems.at[5]))
    copies[-1].start()
    ggv[...] = jnp.sum(wt[...] * total, axis=0, keepdims=True)
    copies.append(pltpu.make_async_copy(ggv, gg_o, sems.at[6]))
    copies[-1].start()
    for copy in copies:
        copy.wait()


def shards(tokens, norm_gain, value_weight, cotangent, pseudo_grad, outer_params, momentum):
    hbm = pl.BlockSpec(memory_space=pl.ANY)
    vmem = pl.BlockSpec(memory_space=pltpu.VMEM)
    out = jax.ShapeDtypeStruct
    held = pl.pallas_call(
        kernel,
        out_shape=(
            pltpu.VMEM((T, K), BF16),
            pltpu.VMEM((T, D), BF16),
            pltpu.VMEM((K, B), F32),
            pltpu.VMEM((K1, B), BF16),
            pltpu.VMEM((K1, B), BF16),
            pltpu.VMEM((K1, B), BF16),
            pltpu.VMEM((K2, B), BF16),
            pltpu.VMEM((K, B), F32),
            pltpu.VMEM((ROWS, SHARE), F32),
            pltpu.VMEM((ROWS, SHARE), F32),
            pltpu.VMEM((ROWS, D), BF16),
            pltpu.VMEM((1, B), BF16),
        ),
        in_specs=[hbm] * 7,
        out_specs=(vmem,) * 12,
        scratch_shapes=[
            pltpu.VMEM((8, T, B), BF16),
            pltpu.VMEM((N_FSDP, B, K), BF16),
            pltpu.VMEM((2, 4, K, B), BF16),
            pltpu.VMEM((3, K1, B), BF16),
            pltpu.VMEM((3, M1, B), BF16),
            pltpu.VMEM((3, M1, B), BF16),
            pltpu.VMEM((2, K2, B), BF16),
            pltpu.VMEM((2, K2, B), BF16),
            pltpu.VMEM((B, K), BF16),
            pltpu.VMEM((T, K), BF16),
            pltpu.VMEM((T, K), BF16),
            pltpu.VMEM((2, K, T), BF16),
            pltpu.VMEM((T, K), F32),
            pltpu.VMEM((T, 128), F32),
            pltpu.VMEM((T, 1), F32),
            pltpu.VMEM((PARTS, 3, PR, 2 * SHARE), BF16),
            pltpu.VMEM((ROWS, 2 * SHARE), BF16),
            pltpu.VMEM((PARTS, PR, SHARE), BF16),
            pltpu.VMEM((PARTS, PR, SHARE), BF16),
            pltpu.VMEM((PARTS, PR, SHARE), F32),
            pltpu.VMEM((ROWS, SHARE), F32),
            pltpu.VMEM((ROWS, SHARE), F32),
            pltpu.SemaphoreType.DMA((N_COPIES,)),
            pltpu.SemaphoreType.DMA((N_COPIES,)),
            pltpu.SemaphoreType.DMA((16,)),
        ],
        compiler_params=pltpu.CompilerParams(
            collective_id=0, has_side_effects=True, vmem_limit_bytes=40 << 20
        ),
        name="window",
    )(tokens, norm_gain, value_weight, cotangent, pseudo_grad, outer_params, momentum)
    held = [pltpu.with_memory_space_constraint(v, pltpu.VMEM) for v in held]
    return tuple(
        pl.pallas_call(
            finish,
            out_shape=(
                out((T, K), BF16),
                out((T, D), BF16),
                out((1, B, K), F32),
                out((1, B), F32),
                out((ROWS, SHARE), F32),
                out((ROWS, SHARE), F32),
                out((ROWS, D), BF16),
            ),
            in_specs=[vmem] * 12,
            out_specs=(hbm,) * 7,
            scratch_shapes=[
                pltpu.VMEM((B, K), F32),
                pltpu.VMEM((1, B), F32),
                pltpu.SemaphoreType.DMA((8,)),
            ],
            compiler_params=pltpu.CompilerParams(vmem_limit_bytes=16 << 20),
            name="finish",
        )(*held)
    )


def solution(mesh):
    placed = (
        P(("group", "fsdp"), None),
        P("group", "fsdp"),
        P("group", "fsdp", None),
        P(("group", "fsdp"), None),
        P("group", "fsdp", None),
        P("fsdp", "group"),
        P("fsdp", "group"),
    )
    return jax.shard_map(
        shards,
        mesh=mesh,
        in_specs=placed,
        out_specs=(
            P(("group", "fsdp"), None),
            P(("group", "fsdp"), None),
            P("group", "fsdp", None),
            P("group", "fsdp"),
            P("fsdp", "group"),
            P("fsdp", "group"),
            P("fsdp", None),
        ),
        check_vma=False,
    )
```
